128 devices in a mesh: dp: 16 (over z, y_hi, core), expert: 8 (over y_lo, x).
Axes of the slice: x: 4, y: 4 (y_hi: 2, y_lo: 2; y = y_hi * 2 + y_lo), z: 4, core: 2. Of those that a mesh axis runs over, the one named last changes fastest.
Arguments:
- tokens: bfloat16 [1536, 6144], P(('dp', 'expert')), may hold values from -6 to 6
- cotangent: bfloat16 [1536, 6144], P(('dp', 'expert')), may hold values from -6 to 6
- expert_ids: int32 [1536, 2], P('dp'), may hold values from 0 to 7, all different within a row; in each aligned block of 96 rows (0 to 95, 96 to 191, ...) at most 32 rows name the same one
- gate_values: float32 [1536, 2], P('dp'), may hold values from 0.2 to 1
- w_in: bfloat16 [8, 6144, 8192], P('expert', None, 'dp'), may hold values from -0.078125 to 0.078125
- w_out: bfloat16 [8, 8192, 6144], P('expert', 'dp'), may hold values from -0.0625 to 0.0625
Outputs:
- layer_out: bfloat16 [1536, 6144], P(('dp', 'expert'))
- grad_tokens: bfloat16 [1536, 6144], P(('dp', 'expert'))
- grad_in: bfloat16 [8, 6144, 8192], P('expert', None, 'dp')
- grad_out: bfloat16 [8, 8192, 6144], P('expert', 'dp')
The draws below stay inside these ranges and needn't reach their ends.
Inputs may be any that keep to these rules, and one draw needn't show every extreme that they name: `expert_ids`: A token names 2 different experts. Within the 96 tokens of one dp index no expert is named by more than 32 tokens, and in every draw some expert is named by exactly 32 tokens of some dp index.
All inputs are finite; a program needn't handle non-finite values.
Results may differ from the reference program's by a relative error of at most 0.0058.
Values may be sent and summed in bfloat16 or wider, within the bound.
A program may use at most 192 MiB of HBM per device.

```python
import math
import jax
import jax.numpy as jnp
import numpy as np
from jax import lax

D = 6144
TOP = 2
TOK_DP = 96
CAP = 32
EXPERTS = 8
FF = 8192
TOKENS = 1536
N_DP = 16


def steps_of(stream_key, shape, split, smallest, high):
    loudness = 1.0
    for dim, shards_of in split:
        steps = jax.random.uniform(jax.random.fold_in(jax.random.fold_in(stream_key, 6), dim), (shards_of,), jnp.float32, smallest / len(split), high / len(split))
        loudness = loudness * jnp.repeat(jnp.exp(steps), shape[dim] // shards_of).reshape((-1,) + (1,) * (len(shape) - 1 - dim))
    return loudness


def assign_block(own_key, own, number, rows, count, top, limit, slope):
    sequence = jax.random.permutation(own_key, count)
    crowded, common = load_shares(count, rows * top, limit, slope, True), load_shares(count, rows * top, limit, slope, False)
    places = jnp.arange(count)

    def named(sizes, rotation):
        used = int((sizes > 0).sum())
        fixed = max(1, used // 4)
        passed = fixed + (places - fixed + rotation * (used - fixed)) % max(1, count - fixed)
        return jnp.zeros((count,), jnp.int32).at[sequence[jnp.where(places < fixed, places, passed)]].set(jnp.asarray(sizes, jnp.int32))

    sizes = jnp.where(number % 4 == 0, named(crowded, number // 4), named(common, number - number // 4 - 1))
    mixed = jax.random.permutation(jax.random.fold_in(own, 3), count)
    donor, receiver = mixed[0:count // 2 * 2:2], mixed[1:count // 2 * 2:2]
    margin = jnp.minimum(sizes[donor] - 1, limit - sizes[receiver]) // 2
    margin = jnp.where((donor == sequence[0]) | (receiver == sequence[0]) | (sizes[receiver] == 0), 0, jnp.maximum(margin, 0))
    passed = jax.random.randint(jax.random.fold_in(own, 4), (count // 2,), 0, 1 << 20) % (margin + 1)
    sizes = sizes.at[donor].add(-passed).at[receiver].add(passed)
    members = jnp.searchsorted(jnp.cumsum(sizes), jnp.arange(rows * top), side="right").astype(jnp.int32)
    grid = members.reshape(top, rows).T
    grid = grid[jax.random.permutation(jax.random.fold_in(own, 1), rows)]
    rotation = jax.random.randint(jax.random.fold_in(own, 2), (rows, 1), 0, top)
    return jnp.take_along_axis(grid, (jnp.arange(top)[None, :] + rotation) % top, axis=1)


def load_shares(count, total, reach, lean, full):
    weights = [(1 << 20) // math.isqrt(grade ** lean) + 1 for grade in range(1, count + 1)]
    largest = reach if full else min(reach, max(-(-total // count), total * weights[0] // sum(weights)))
    least = 1 if total - largest >= count - 1 else 0
    counts, spare = [largest] + [least] * (count - 1), total - largest - least * (count - 1)
    while spare > 0:
        candidates = [i for i in range(1, count) if counts[i] < largest] or [i for i in range(1, count) if counts[i] < reach]
        whole, budget = sum([weights[i] for i in candidates]), spare
        for i in candidates:
            addition = min(reach - counts[i], max(1, budget * weights[i] // whole), spare)
            counts[i] = counts[i] + addition
            spare = spare - addition
    return np.array(counts)


def centred(rng, extent, deviation, most, pieces=(), held_as=jnp.bfloat16):
    entries = jax.random.normal(rng, extent, jnp.float32) * deviation
    if len(pieces) > 0:
        entries = steps_of(rng, extent, pieces, -0.22, 0.18) * entries
    return jnp.clip(entries, min=-most, max=most).astype(held_as)


def setup_inputs(seed: int = 0) -> dict:
    keys = jax.random.split(jax.random.key(seed), 7)
    tokens = centred(keys[0], (TOKENS, D), 1.0, 6.0, ((0, 128),))
    cotangent = centred(keys[1], (TOKENS, D), 1.0, 6.0, ((0, 128),))
    expert_ids_keys = jax.random.split(jax.random.fold_in(keys[2], 1), TOKENS // TOK_DP)
    expert_ids_turns = jax.random.permutation(jax.random.fold_in(keys[2], 3), TOKENS // TOK_DP)
    expert_ids = jax.vmap(lambda own, number: assign_block(jax.random.fold_in(keys[2], 2), own, number, TOK_DP, EXPERTS, TOP, CAP, 2))(expert_ids_keys, expert_ids_turns).reshape((TOKENS, TOP))
    gate_values = jnp.clip(0.2 + 0.8 * jax.random.uniform(keys[3], (TOKENS, TOP), jnp.float32) ** steps_of(keys[3], (TOKENS, TOP), ((0, 16),), -0.2, 0.2), 0.2, 1.0)
    w_in = centred(keys[4], (EXPERTS, D, FF), D ** -0.5, 0.078125, ((0, 8), (2, 16)))
    w_out = centred(keys[5], (EXPERTS, FF, D), FF ** -0.5, 0.0625, ((0, 8), (1, 16)))
    return dict(tokens=tokens, cotangent=cotangent, expert_ids=expert_ids, gate_values=gate_values, w_in=w_in, w_out=w_out)


def slot_tables(ids, gates, expert):
    chosen = ids == expert
    gate_sum = jnp.sum(jnp.where(chosen, gates, jnp.float32(0.0)), axis=1)
    picked = jnp.any(chosen, axis=1).astype(jnp.int32)
    placed = jnp.cumsum(picked) - 1
    slots = lax.broadcasted_iota(jnp.int32, (CAP, TOK_DP), 0)
    table = ((placed[None, :] == slots) & (picked[None, :] == 1)).astype(jnp.float32)
    return table, gate_sum


def reference(tokens, cotangent, expert_ids, gate_values, w_in, w_out):
    tok_groups = tokens.reshape(N_DP, TOK_DP, D).astype(jnp.float32)
    cot_groups = cotangent.reshape(N_DP, TOK_DP, D).astype(jnp.float32)
    id_groups = expert_ids.reshape(N_DP, TOK_DP, TOP)
    gate_groups = gate_values.reshape(N_DP, TOK_DP, TOP)
    out_total = jnp.zeros((N_DP, TOK_DP, D), jnp.float32)
    back_total = jnp.zeros((N_DP, TOK_DP, D), jnp.float32)
    grads_in = []
    grads_out = []
    highest = lax.Precision.HIGHEST
    for expert in range(EXPERTS):
        tables, gate_sum = jax.vmap(lambda i, g: slot_tables(i, g, expert))(id_groups, gate_groups)
        rows = jnp.einsum("gct,gtd->gcd", tables, tok_groups, precision=highest).astype(jnp.bfloat16).reshape(N_DP * CAP, D)
        pre = jnp.dot(rows, w_in[expert], preferred_element_type=jnp.float32)
        hidden = jax.nn.silu(pre).astype(jnp.bfloat16)
        slot_out = jnp.dot(hidden, w_out[expert], preferred_element_type=jnp.float32).reshape(N_DP, CAP, D)
        out_total = out_total + gate_sum[..., None] * jnp.einsum("gct,gcd->gtd", tables, slot_out, precision=highest)
        weighted = (gate_sum[..., None] * cot_groups).astype(jnp.bfloat16).astype(jnp.float32)
        slot_grad = jnp.einsum("gct,gtd->gcd", tables, weighted, precision=highest).astype(jnp.bfloat16).reshape(N_DP * CAP, D)
        grads_out.append(jnp.dot(hidden.T, slot_grad, preferred_element_type=jnp.float32).astype(jnp.bfloat16))
        grad_hidden = jnp.dot(slot_grad, w_out[expert].T, preferred_element_type=jnp.float32)
        sig = jax.nn.sigmoid(pre)
        grad_pre = (grad_hidden * sig * (1.0 + pre * (1.0 - sig))).astype(jnp.bfloat16)
        grads_in.append(jnp.dot(rows.T, grad_pre, preferred_element_type=jnp.float32).astype(jnp.bfloat16))
        slot_back = jnp.dot(grad_pre, w_in[expert].T, preferred_element_type=jnp.float32).reshape(N_DP, CAP, D)
        back_total = back_total + jnp.einsum("gct,gcd->gtd", tables, slot_back, precision=highest)
    layer_out = out_total.reshape(TOKENS, D).astype(jnp.bfloat16)
    grad_tokens = back_total.reshape(TOKENS, D).astype(jnp.bfloat16)
    return layer_out, grad_tokens, jnp.stack(grads_in), jnp.stack(grads_out)
```

```python
import functools
import jax
import jax.numpy as jnp
from jax import lax
from jax.experimental import pallas as pl
from jax.experimental.pallas import tpu as pltpu
from jax.sharding import PartitionSpec as P

D = 6144
HID = 512
CAP = 32
TOK = 96
NC = 6
CW = D // NC
QW = CW // 4
ROWS = 512
HALF = 256
DEP = 4
LAG4, LAG5, LAG6 = 1, 2, 3
OFF = NC + LAG6
L2, L3, L4, L5, L6 = 1, 2, 3, 4, 5
STEPS = OFF + 2 * NC + L6
MESH = pl.DeviceIdType.MESH
F32, BF16 = jnp.float32, jnp.bfloat16


def rem(a, b):
    return lax.rem(a, jnp.int32(b))


def at16(v, m=32):
    return pl.multiple_of(v, m)


def dot(a, b, dims=((1,), (0,)), precision=None):
    return lax.dot_general(a, b, (dims, ((), ())), precision=precision, preferred_element_type=F32)


def done(ref, sem):
    pltpu.make_async_copy(ref, ref, sem).wait()


def exchange(
    x_ref, ids_ref, gates_ref, win_hbm, wout_hbm,
    out_ref, rg_hbm, hid, gp,
    win, wout, G, R, pre, gh, A, grep, gslot,
    SB, PO, RB, SS, Z2, Z1, YS, YR, TF, EB, ER,
    w_sem, ge_s, ge_r, ag_s, y_r, zm_r, zp_r, z2m_r, z2p_r, sib_r, hbm_s,
    sb_s, rb_r, ss_s, rz2m_r, rz2p_r, rz1m_r, rz1p_r, ys_s, yr_r, eb_s, er_r,
):
    dp, e = lax.axis_index("dp"), lax.axis_index("expert")
    z, yh, c = dp // 4, (dp // 2) % 2, dp % 2

    def at(zz, yy, cc):
        return (zz * 4 + yy * 2 + cc, e)

    zn, zp_, zo = rem(z + 1, 4), rem(z + 3, 4), rem(z + 2, 4)
    up, down, across, sib = at(zn, yh, c), at(zp_, yh, c), at(z, 1 - yh, c), at(z, yh, 1 - c)
    peers = [rem(e + d, 8) for d in range(1, 8)]

    def send(src, dst, ss, rs, to):
        pltpu.make_async_remote_copy(
            src_ref=src, dst_ref=dst, send_sem=ss, recv_sem=rs, device_id=to, device_id_type=MESH
        ).start()

    load_in = pltpu.make_async_copy(win_hbm, win, w_sem.at[0])
    load_out = pltpu.make_async_copy(wout_hbm, wout, w_sem.at[1])
    load_in.start()
    load_out.start()

    barrier = pltpu.get_barrier_semaphore()
    for to in [up, down, across, sib] + [(dp, p) for p in peers]:
        pl.semaphore_signal(barrier, inc=1, device_id=to, device_id_type=MESH)
    pl.semaphore_wait(barrier, 11)

    mine = pl.ds(at16(e * 48, 16), 48)

    def a1(g):
        for p in peers:
            send(x_ref.at[g], G.at[g, mine], ge_s.at[g], ge_r.at[g], (dp, p))
        G[g, mine] = x_ref[g]

    a1(0)
    a1(1)

    chosen = ids_ref[...] == e
    gsum = jnp.sum(jnp.where(chosen, gates_ref[...], 0.0), axis=1, keepdims=True)
    picked = jnp.max(jnp.where(chosen, 1.0, 0.0), axis=1, keepdims=True)
    row = lax.broadcasted_iota(jnp.int32, (TOK, TOK), 0)
    col = lax.broadcasted_iota(jnp.int32, (TOK, TOK), 1)
    tri = jnp.where(row >= col, 1.0, 0.0).astype(BF16)
    pickb = jnp.broadcast_to(picked, (TOK, 128))
    place = dot(tri, pickb.astype(BF16)) - 1.0
    slots = lax.broadcasted_iota(jnp.int32, (TOK, 128), 1)
    spread = jnp.bitwise_and(slots, 31).astype(F32)
    table = jnp.where(place == spread, pickb, 0.0)
    r4 = lax.broadcasted_iota(jnp.int32, (4 * TOK, TOK), 0)
    t4 = lax.broadcasted_iota(jnp.int32, (4 * TOK, TOK), 1)
    widen = jnp.where(jnp.right_shift(r4, 2) == t4, 1.0, 0.0)
    q_r = jnp.bitwise_and(lax.broadcasted_iota(jnp.int32, (4 * TOK, 128), 0), 3)
    q_c = jnp.right_shift(lax.broadcasted_iota(jnp.int32, (4 * TOK, 128), 1), 5)
    wide = dot(widen.astype(BF16), table.astype(BF16))
    A[...] = jnp.where(q_r == q_c, wide, 0.0).astype(BF16)
    gsb = jnp.broadcast_to(gsum, (TOK, 128))
    grep[...] = dot(widen, gsb, precision=lax.Precision.HIGHEST)
    gslot[...] = dot(table, gsb, ((0,), (0,)), precision=lax.Precision.HIGHEST)

    pre[...] = jnp.zeros_like(pre)
    gh[...] = jnp.zeros_like(gh)

    def block(zz, yy, n=32):
        return pl.ds(at16((c * 8 + zz * 2 + yy) * 32), n)

    def to_sib(g, where):
        send(R.at[g, where], R.at[g, where], ag_s.at[g], sib_r.at[g], sib)

    def a2(g):
        done(G.at[g, pl.ds(0, 336)], ge_r.at[g])
        scale = jnp.where(g < NC, 1.0, grep[...][:, :1])
        v = (G[g].astype(F32) * scale).astype(BF16)
        packed = dot(A[...], v, ((0,), (0,))).astype(BF16)
        own = block(z, yh)
        for q in range(4):
            R[g, own, q * QW : (q + 1) * QW] = packed[q * 32 : (q + 1) * 32]
        me = R.at[g, own]
        send(me, me, ag_s.at[g], y_r.at[g], across)
        send(me, me, ag_s.at[g], zm_r.at[g], up)
        send(me, me, ag_s.at[g], zp_r.at[g], down)
        to_sib(g, own)

    def a3(g):
        theirs = block(z, 1 - yh)
        b = R.at[g, theirs]
        done(b, y_r.at[g])
        send(b, b, ag_s.at[g], zm_r.at[g], up)
        send(b, b, ag_s.at[g], zp_r.at[g], down)
        to_sib(g, theirs)

    def a4(g):
        low = block(zp_, 0, 64)
        done(R.at[g, low], zm_r.at[g])
        b = R.at[g, block(zp_, 0)]
        send(b, b, ag_s.at[g], z2m_r.at[g], up)
        to_sib(g, low)
        high = block(zn, 0, 64)
        done(R.at[g, high], zp_r.at[g])
        b = R.at[g, block(zn, 1)]
        send(b, b, ag_s.at[g], z2p_r.at[g], down)
        to_sib(g, high)

    def a5(g):
        done(R.at[g, block(zo, 0)], z2m_r.at[g])
        done(R.at[g, block(zo, 1)], z2p_r.at[g])
        to_sib(g, block(zo, 0, 64))

    def a6(g):
        done(R.at[g, pl.ds(at16((1 - c) * HALF), HALF)], sib_r.at[g])
        pltpu.make_async_copy(R.at[g], rg_hbm.at[g], hbm_s.at[g]).start()

        @pl.when(g == 0)
        def _():
            load_in.wait()
            load_out.wait()

        @pl.when(g < NC)
        def _():
            pre[...] += dot(R[g], win[pl.ds(at16(g * CW, CW), CW), :])

        @pl.when(g >= NC)
        def _():
            gh[...] += dot(R[g], wout[:, pl.ds(at16((g - NC) * CW, CW), CW)], ((1,), (1,)))

        @pl.when(g == NC - 1)
        def _():
            v = pre[...]
            hid[...] = (v * jax.nn.sigmoid(v)).astype(BF16)

        @pl.when(g == 2 * NC - 1)
        def _():
            v = pre[...]
            s = jax.nn.sigmoid(v)
            gp[...] = (gh[...] * s * (1.0 + v * (1.0 - s))).astype(BF16)

    ours, others = pl.ds(at16(c * HALF), HALF), pl.ds(at16((1 - c) * HALF), HALF)

    def c1(h):
        two, slot = rem(h, 2), rem(h, DEP)

        @pl.when(h >= 2)
        def _():
            done(SB.at[two], sb_s.at[two])

        def product(lhs, w, dims):
            SB[two] = dot(lhs[others, :], w, dims).astype(BF16)
            send(SB.at[two], RB.at[slot], sb_s.at[two], rb_r.at[slot], sib)
            PO[...] = dot(lhs[ours, :], w, dims)

        @pl.when(h < NC)
        def _():
            product(hid, wout[:, pl.ds(at16(h * CW, CW), CW)], ((1,), (0,)))

        @pl.when(h >= NC)
        def _():
            product(gp, win[pl.ds(at16((h - NC) * CW, CW), CW), :], ((1,), (1,)))

    def part(zz, yy, n=32):
        return pl.ds(at16((zz * 2 + yy) * 32), n)

    def c2(h):
        slot = rem(h, DEP)

        @pl.when(h >= DEP)
        def _():
            done(SS.at[slot, pl.ds(0, 192)], ss_s.at[slot])

        done(RB.at[slot], rb_r.at[slot])
        SS[slot] = (PO[...] + RB[slot].astype(F32)).astype(BF16)
        s = ss_s.at[slot]
        send(SS.at[slot, part(zo, 0)], Z2.at[slot, 0], s, rz2m_r.at[slot], up)
        send(SS.at[slot, part(zo, 1)], Z2.at[slot, 1], s, rz2p_r.at[slot], down)
        send(SS.at[slot, part(zn, 1)], Z1.at[slot, 0, pl.ds(32, 32)], s, rz1m_r.at[slot], up)
        send(SS.at[slot, part(zp_, 0)], Z1.at[slot, 1, pl.ds(0, 32)], s, rz1p_r.at[slot], down)

    def c3(h):
        slot = rem(h, DEP)
        s = ss_s.at[slot]
        done(Z2.at[slot, 0], rz2m_r.at[slot])
        b = part(zn, 0)
        SS[slot, b] = (SS[slot, b].astype(F32) + Z2[slot, 0].astype(F32)).astype(BF16)
        send(SS.at[slot, b], Z1.at[slot, 0, pl.ds(0, 32)], s, rz1m_r.at[slot], up)
        done(Z2.at[slot, 1], rz2p_r.at[slot])
        b = part(zp_, 1)
        SS[slot, b] = (SS[slot, b].astype(F32) + Z2[slot, 1].astype(F32)).astype(BF16)
        send(SS.at[slot, b], Z1.at[slot, 1, pl.ds(32, 32)], s, rz1p_r.at[slot], down)

    def c4(h):
        slot = rem(h, DEP)

        @pl.when(h >= DEP)
        def _():
            done(YS.at[slot], ys_s.at[slot])

        done(Z1.at[slot, 0], rz1m_r.at[slot])
        done(Z1.at[slot, 1], rz1p_r.at[slot])

        def total(yy):
            b = pl.ds(at16(yy * 32), 32)
            return SS[slot, part(z, yy)].astype(F32) + Z1[slot, 0, b].astype(F32) + Z1[slot, 1, b].astype(F32)

        YS[slot] = total(1 - yh).astype(BF16)
        send(YS.at[slot], YR.at[slot], ys_s.at[slot], yr_r.at[slot], across)
        TF[...] = total(yh)

    def c5(h):
        slot = rem(h, DEP)

        @pl.when(h >= DEP)
        def _():
            done(EB.at[slot, pl.ds(0, 336)], eb_s.at[slot])

        done(YR.at[slot], yr_r.at[slot])
        scale = jnp.where(h < NC, gslot[pl.ds(0, 32), :][:, :1], 1.0)
        v = ((TF[...] + YR[slot].astype(F32)) * scale).astype(BF16)
        v = jnp.concatenate([v[:, q * QW : (q + 1) * QW] for q in range(4)], axis=0)
        EB[slot] = dot(A[...], v).astype(BF16)
        for p in peers:
            send(EB.at[slot, pl.ds(at16(p * 48, 16), 48)], ER.at[slot, mine], eb_s.at[slot], er_r.at[slot], (dp, p))
        ER[slot, mine] = EB[slot, mine]

    def c6(h):
        slot = rem(h, DEP)
        done(ER.at[slot, pl.ds(0, 336)], er_r.at[slot])
        t = ER[slot, 0:48].astype(F32)
        for j in range(1, 8):
            t = t + ER[slot, 48 * j : 48 * j + 48].astype(F32)
        out_ref[h] = t.astype(BF16)

    def stage(f, i, n=2 * NC):
        @pl.when((i >= 0) & (i < n))
        def _():
            f(i)

    def step(t, carry):
        stage(a1, jnp.where(t + 2 < 2 * NC, t + 2, -1))
        stage(a2, t)
        stage(a4, t - LAG4)
        stage(a3, t)
        stage(a5, t - LAG5)
        stage(a6, t - LAG6)
        h = t - OFF
        stage(c6, h - L6)
        stage(c5, h - L5)
        stage(c4, h - L4)
        stage(c3, h - L3)
        stage(c2, h - L2)
        stage(c1, h)
        return carry

    lax.fori_loop(0, STEPS, step, 0)

    def finish(g, carry):
        done(G.at[g, pl.ds(0, 336)], ge_s.at[g])
        done(R.at[g, pl.ds(0, 480)], ag_s.at[g])
        pltpu.make_async_copy(R.at[g], rg_hbm.at[g], hbm_s.at[g]).wait()
        return carry

    lax.fori_loop(0, 2 * NC, finish, 0)
    for i in range(2):
        done(SB.at[i], sb_s.at[i])
    for i in range(DEP):
        done(SS.at[i, pl.ds(0, 192)], ss_s.at[i])
        done(YS.at[i], ys_s.at[i])
        done(EB.at[i, pl.ds(0, 336)], eb_s.at[i])


def grads(rows, slot_grad, hid, gp, gin, gout):
    gin[...] = dot(rows[0], gp[...], ((0,), (0,))).astype(BF16)
    gout[...] = dot(hid[...], slot_grad[0], ((0,), (0,))).astype(BF16)


def local(tokens, cotangent, expert_ids, gate_values, w_in, w_out):
    both = jnp.stack([tokens, cotangent])
    x = both.reshape(2, 12, NC, 4, QW).transpose(0, 2, 1, 3, 4).reshape(2 * NC, 48, QW)
    vmem, hbm = pl.BlockSpec(memory_space=pltpu.VMEM), pl.BlockSpec(memory_space=pl.ANY)
    dma = lambda n: pltpu.SemaphoreType.DMA((n,))
    out, rg, hid, gp = pl.pallas_call(
        exchange,
        name="exchange",
        out_shape=(
            jax.ShapeDtypeStruct((2 * NC, 48, QW), BF16),
            jax.ShapeDtypeStruct((2 * NC, ROWS, CW), BF16),
            jax.ShapeDtypeStruct((ROWS, HID), BF16),
            jax.ShapeDtypeStruct((ROWS, HID), BF16),
        ),
        in_specs=[vmem, vmem, vmem, hbm, hbm],
        out_specs=(vmem, hbm, vmem, vmem),
        scratch_shapes=[
            pltpu.VMEM((D, HID), BF16),
            pltpu.VMEM((HID, D), BF16),
            pltpu.VMEM((2 * NC, 4 * TOK, QW), BF16),
            pltpu.VMEM((2 * NC, ROWS, CW), BF16),
            pltpu.VMEM((ROWS, HID), F32),
            pltpu.VMEM((ROWS, HID), F32),
            pltpu.VMEM((4 * TOK, 128), BF16),
            pltpu.VMEM((4 * TOK, 128), F32),
            pltpu.VMEM((128, 128), F32),
            pltpu.VMEM((2, HALF, CW), BF16),
            pltpu.VMEM((HALF, CW), F32),
            pltpu.VMEM((DEP, HALF, CW), BF16),
            pltpu.VMEM((DEP, HALF, CW), BF16),
            pltpu.VMEM((DEP, 2, 32, CW), BF16),
            pltpu.VMEM((DEP, 2, 64, CW), BF16),
            pltpu.VMEM((DEP, 32, CW), BF16),
            pltpu.VMEM((DEP, 32, CW), BF16),
            pltpu.VMEM((32, CW), F32),
            pltpu.VMEM((DEP, 4 * TOK, QW), BF16),
            pltpu.VMEM((DEP, 4 * TOK, QW), BF16),
            dma(2),
        ]
        + [dma(2 * NC) for _ in range(10)]
        + [dma(2), dma(DEP), dma(DEP)]
        + [dma(DEP) for _ in range(8)],
        compiler_params=pltpu.CompilerParams(
            collective_id=0, has_side_effects=True, vmem_limit_bytes=56 * 2**20
        ),
    )(x, expert_ids, gate_values, w_in[0], w_out[0])
    one = lambda f: pl.BlockSpec((1, ROWS, CW), f)
    grad_in, grad_out = pl.pallas_call(
        grads,
        name="grads",
        grid=(NC,),
        out_shape=(
            jax.ShapeDtypeStruct((D, HID), BF16),
            jax.ShapeDtypeStruct((HID, D), BF16),
        ),
        in_specs=[
            one(lambda k: (k, 0, 0)),
            one(lambda k: (NC + k, 0, 0)),
            pl.BlockSpec((ROWS, HID), lambda k: (0, 0)),
            pl.BlockSpec((ROWS, HID), lambda k: (0, 0)),
        ],
        out_specs=(
            pl.BlockSpec((CW, HID), lambda k: (k, 0)),
            pl.BlockSpec((HID, CW), lambda k: (0, k)),
        ),
        compiler_params=pltpu.CompilerParams(vmem_limit_bytes=40 * 2**20),
    )(rg, rg, hid, gp)
    final = out.reshape(2, NC, 12, 4, QW).transpose(0, 2, 1, 3, 4).reshape(2, 12, D)
    return final[0], final[1], grad_in[None], grad_out[None]


def solution(mesh):
    placed = (
        P(("dp", "expert"), None),
        P(("dp", "expert"), None),
        P("dp", None),
        P("dp", None),
        P("expert", None, "dp"),
        P("expert", "dp", None),
    )
    return jax.shard_map(
        local,
        mesh=mesh,
        in_specs=placed,
        out_specs=(
            P(("dp", "expert"), None),
            P(("dp", "expert"), None),
            P("expert", None, "dp"),
            P("expert", "dp", None),
        ),
        check_vma=False,
    )
```

```python
import functools
import jax
import jax.numpy as jnp
from jax import lax
from jax.experimental import pallas as pl
from jax.experimental.pallas import tpu as pltpu
from jax.sharding import PartitionSpec as P

D = 6144
HID = 512
CAP = 32
TOK = 96
NC = 6
CW = D // NC
QW = CW // 4
ROWS = 512
HALF = 256
DEP = 6
MOD, WHICH = 3, 2
LEAD = 3
LAG3, LAG4, LAG5, LAGY, LAG6 = 1, 3, 5, 6, 7
OFF = NC + LAG6
L2, L3, L4, L5, L6, L7 = 1, 3, 5, 7, 9, 11
STEPS = OFF + 2 * NC + L7
MESH = pl.DeviceIdType.MESH
F32, BF16 = jnp.float32, jnp.bfloat16


def rem(a, b):
    return lax.rem(a, jnp.int32(b))


def at16(v, m=32):
    return pl.multiple_of(v, m)


def dot(a, b, dims=((1,), (0,)), precision=None):
    return lax.dot_general(a, b, (dims, ((), ())), precision=precision, preferred_element_type=F32)


def y_first(i):
    return i % MOD == WHICH if isinstance(i, int) else rem(i, MOD) == WHICH


def done(ref, sem):
    pltpu.make_async_copy(ref, ref, sem).wait()


def exchange(
    tok_ref, cot_ref, ids_ref, gates_ref, win_hbm, wout_hbm,
    lo_ref, gt_ref, rg_hbm, hid, gp,
    win, wout, X, G, R, pre, gh, A, grep, gslot,
    SB, PO, RB, SS, Z2, Z1, YB, YS, YR, TF, EB, ER, FB, FR, FT,
    w_sem, ge_s, ge_r, gp_r, ag_s, y_r, zm_r, zp_r, z2m_r, z2p_r, sib_r, hbm_s,
    sb_s, rb_r, ss_s, ry_r, rz2m_r, rz2p_r, rz1m_r, rz1p_r, ys_s, yr_r, eb_s, er_r, fb_s, fr_r,
):
    dp, e = lax.axis_index("dp"), lax.axis_index("expert")
    z, yh, c = dp // 4, (dp // 2) % 2, dp % 2
    yl, x = e // 4, e % 4

    def at(zz, yy, cc):
        return (zz * 4 + yy * 2 + cc, e)

    zn, zp_, zo = rem(z + 1, 4), rem(z + 3, 4), rem(z + 2, 4)
    up, down, across, sib = at(zn, yh, c), at(zp_, yh, c), at(z, 1 - yh, c), at(z, yh, 1 - c)
    xs = [rem(x + d, 4) for d in range(1, 4)]
    peers = [(dp, yl * 4 + p) for p in xs]
    pair = (dp, (1 - yl) * 4 + x)

    def send(src, dst, ss, rs, to):
        pltpu.make_async_remote_copy(
            src_ref=src, dst_ref=dst, send_sem=ss, recv_sem=rs, device_id=to, device_id_type=MESH
        ).start()

    load_in = pltpu.make_async_copy(win_hbm, win, w_sem.at[0])
    load_out = pltpu.make_async_copy(wout_hbm, wout, w_sem.at[1])
    load_in.start()
    load_out.start()

    barrier = pltpu.get_barrier_semaphore()
    for to in [up, down, across, sib, pair] + peers:
        pl.semaphore_signal(barrier, inc=1, device_id=to, device_id_type=MESH)
    pl.semaphore_wait(barrier, 8)

    mine = pl.ds(at16((x * 2 + yl) * 48, 16), 48)
    twin = pl.ds(at16((x * 2 + 1 - yl) * 48, 16), 48)

    def quarters(v):
        return jnp.concatenate([v[:, q * QW : (q + 1) * QW] for q in range(4)], axis=0)

    def a1(g):
        k = jnp.where(g < NC, g, g - NC)
        where = pl.ds(at16(k * CW, CW), CW)
        v = jnp.where(g < NC, tok_ref[:, where].astype(F32), cot_ref[:, where].astype(F32))
        v = quarters(v).astype(BF16)
        X[g] = v
        G[g, mine] = v
        send(X.at[g], G.at[g, mine], ge_s.at[g], gp_r.at[g], pair)
        for to in peers:
            send(X.at[g], G.at[g, mine], ge_s.at[g], ge_r.at[g], to)

    def a1b(g):
        b = G.at[g, twin]
        done(b, gp_r.at[g])
        for to in peers:
            send(b, b, ge_s.at[g], ge_r.at[g], to)

    for g in range(LEAD):
        a1(jnp.int32(g))

    chosen = ids_ref[...] == e
    gsum = jnp.sum(jnp.where(chosen, gates_ref[...], 0.0), axis=0, keepdims=True)
    picked = jnp.max(jnp.where(chosen, 1.0, 0.0), axis=0, keepdims=True)
    row = lax.broadcasted_iota(jnp.int32, (TOK, TOK), 0)
    col = lax.broadcasted_iota(jnp.int32, (TOK, TOK), 1)
    tri = jnp.where(row <= col, 1.0, 0.0).astype(BF16)
    pickb = jnp.broadcast_to(picked, (128, TOK))
    place = dot(pickb.astype(BF16), tri) - 1.0
    slots = jnp.bitwise_and(lax.broadcasted_iota(jnp.int32, (128, TOK), 0), 31).astype(F32)
    table = jnp.where(place == slots, pickb, 0.0)
    r4 = lax.broadcasted_iota(jnp.int32, (4 * TOK, 128), 0)
    c4_ = lax.broadcasted_iota(jnp.int32, (4 * TOK, 128), 1)
    j4 = jnp.right_shift(r4 * 683, 15)
    rest = r4 - j4 * 48
    q_r = jnp.right_shift(rest * 171, 11)
    token = (jnp.bitwise_and(j4, 1) * 4 + jnp.right_shift(j4, 1)) * 12 + rest - q_r * 12
    q_c = jnp.right_shift(c4_, 5)
    widen = jnp.where(token == c4_, 1.0, 0.0)[:, :TOK]
    nt = ((1,), (1,))
    wide = dot(widen.astype(BF16), table.astype(BF16), nt)
    A[...] = jnp.where(q_r == q_c, wide, 0.0).astype(BF16)
    gsb = jnp.broadcast_to(gsum, (128, TOK))
    grep[...] = dot(widen, gsb, nt, lax.Precision.HIGHEST)
    gslot[...] = dot(table, gsb, nt, lax.Precision.HIGHEST)

    a1b(jnp.int32(0))

    pre[...] = jnp.zeros_like(pre)
    gh[...] = jnp.zeros_like(gh)

    def block(zz, yy, n=32, skip=0):
        return pl.ds(at16((c * 8 + yy * 4 + zz) * 32 + skip, 16), n)

    def to_sib(g, where):
        send(R.at[g, where], R.at[g, where], ag_s.at[g], sib_r.at[g], sib)

    def a2(g):
        done(G.at[g, pl.ds(0, 288)], ge_r.at[g])
        scale = jnp.where(g < NC, 1.0, grep[...][:, :1])
        v = (G[g].astype(F32) * scale).astype(BF16)
        packed = dot(A[...], v, ((0,), (0,))).astype(BF16)
        own = block(z, yh)
        for q in range(4):
            R[g, own, q * QW : (q + 1) * QW] = packed[q * 32 : (q + 1) * 32]
        me = R.at[g, own]
        send(me, me, ag_s.at[g], y_r.at[g], across)
        send(me, me, ag_s.at[g], zm_r.at[g], up)
        send(me, me, ag_s.at[g], zp_r.at[g], down)
        to_sib(g, own)

    def a3(g):
        @pl.when(jnp.logical_not(y_first(g)))
        def _():
            theirs = block(z, 1 - yh)
            b = R.at[g, theirs]
            done(b, y_r.at[g])
            send(b, b, ag_s.at[g], zm_r.at[g], up)
            send(b, b, ag_s.at[g], zp_r.at[g], down)
            to_sib(g, theirs)

    def a4(g):
        def hand_on(zz, sem, sem2, to, pick):
            @pl.when(jnp.logical_not(y_first(g)))
            def _():
                done(R.at[g, pl.ds(0, 64)], sem.at[g])
                b = R.at[g, block(zz, pick)]
                send(b, b, ag_s.at[g], sem2.at[g], to)
                to_sib(g, block(zz, 0))
                to_sib(g, block(zz, 1))

            @pl.when(y_first(g))
            def _():
                whole = R.at[g, block(zz, yh)]
                done(whole, sem.at[g])
                b = R.at[g, block(zz, yh, 16, 16 * pick)]
                send(b, b, ag_s.at[g], sem2.at[g], to)
                send(whole, whole, ag_s.at[g], y_r.at[g], across)
                to_sib(g, block(zz, yh))

        hand_on(zp_, zm_r, z2m_r, up, 0)
        hand_on(zn, zp_r, z2p_r, down, 1)

    def a5(g):
        @pl.when(jnp.logical_not(y_first(g)))
        def _():
            done(R.at[g, block(zo, 0)], z2m_r.at[g])
            done(R.at[g, block(zo, 1)], z2p_r.at[g])
            to_sib(g, block(zo, 0))
            to_sib(g, block(zo, 1))

        @pl.when(y_first(g))
        def _():
            done(R.at[g, block(zo, yh, 16)], z2m_r.at[g])
            done(R.at[g, block(zo, yh, 16, 16)], z2p_r.at[g])
            b = R.at[g, block(zo, yh)]
            send(b, b, ag_s.at[g], y_r.at[g], across)
            to_sib(g, block(zo, yh))

    def ay(g):
        @pl.when(y_first(g))
        def _():
            b = block(0, 1 - yh, 128)
            done(R.at[g, b], y_r.at[g])
            to_sib(g, b)

    def a6(g):
        done(R.at[g, pl.ds(at16((1 - c) * HALF), HALF)], sib_r.at[g])
        pltpu.make_async_copy(R.at[g], rg_hbm.at[g], hbm_s.at[g]).start()

        @pl.when(g == 0)
        def _():
            load_in.wait()
            load_out.wait()

        @pl.when(g < NC)
        def _():
            pre[...] += dot(R[g], win[pl.ds(at16(g * CW, CW), CW), :])

        @pl.when(g >= NC)
        def _():
            gh[...] += dot(R[g], wout[:, pl.ds(at16((g - NC) * CW, CW), CW)], ((1,), (1,)))

        @pl.when(g == NC - 1)
        def _():
            v = pre[...]
            hid[...] = (v * jax.nn.sigmoid(v)).astype(BF16)

        @pl.when(g == 2 * NC - 1)
        def _():
            v = pre[...]
            s = jax.nn.sigmoid(v)
            gp[...] = (gh[...] * s * (1.0 + v * (1.0 - s))).astype(BF16)

    ours, others = pl.ds(at16(c * HALF), HALF), pl.ds(at16((1 - c) * HALF), HALF)

    def c1(h):
        two, slot = rem(h, 2), rem(h, DEP)

        @pl.when(h >= 2)
        def _():
            done(SB.at[two], sb_s.at[two])

        def product(lhs, w, dims):
            SB[two] = dot(lhs[others, :], w, dims).astype(BF16)
            send(SB.at[two], RB.at[slot], sb_s.at[two], rb_r.at[slot], sib)
            PO[...] = dot(lhs[ours, :], w, dims)

        @pl.when(h < NC)
        def _():
            product(hid, wout[:, pl.ds(at16(h * CW, CW), CW)], ((1,), (0,)))

        @pl.when(h >= NC)
        def _():
            product(gp, win[pl.ds(at16((h - NC) * CW, CW), CW), :], ((1,), (1,)))

    def part(zz, yy, n=32, skip=0):
        return pl.ds(at16((yy * 4 + zz) * 32 + skip, 16), n)

    def either(h, z_way, y_way):
        pl.when(jnp.logical_not(y_first(h)))(z_way)
        pl.when(y_first(h))(y_way)

    def sent(slot, i):
        either(
            i,
            lambda: done(SS.at[slot, pl.ds(0, 192)], ss_s.at[slot]),
            lambda: done(SS.at[slot, pl.ds(0, 224)], ss_s.at[slot]),
        )

    def add_into(slot, b, v):
        SS[slot, b] = (SS[slot, b].astype(F32) + v.astype(F32)).astype(BF16)

    def c2(h):
        slot = rem(h, DEP)

        @pl.when(h >= DEP)
        def _():
            sent(slot, h - DEP)

        done(RB.at[slot], rb_r.at[slot])
        SS[slot] = (PO[...] + RB[slot].astype(F32)).astype(BF16)
        s = ss_s.at[slot]

        def z_way():
            send(SS.at[slot, part(zo, 0)], Z2.at[slot, 0], s, rz2m_r.at[slot], up)
            send(SS.at[slot, part(zo, 1)], Z2.at[slot, 1], s, rz2p_r.at[slot], down)
            send(SS.at[slot, part(zn, 1)], Z1.at[slot, 0, pl.ds(32, 32)], s, rz1m_r.at[slot], up)
            send(SS.at[slot, part(zp_, 0)], Z1.at[slot, 1, pl.ds(0, 32)], s, rz1p_r.at[slot], down)

        def y_way():
            send(SS.at[slot, part(0, 1 - yh, 128)], YB.at[slot], s, ry_r.at[slot], across)

        either(h, z_way, y_way)

    def c3(h):
        slot = rem(h, DEP)
        s = ss_s.at[slot]

        def z_way():
            done(Z2.at[slot, 0], rz2m_r.at[slot])
            b = part(zn, 0)
            add_into(slot, b, Z2[slot, 0])
            send(SS.at[slot, b], Z1.at[slot, 0, pl.ds(0, 32)], s, rz1m_r.at[slot], up)
            done(Z2.at[slot, 1], rz2p_r.at[slot])
            b = part(zp_, 1)
            add_into(slot, b, Z2[slot, 1])
            send(SS.at[slot, b], Z1.at[slot, 1, pl.ds(32, 32)], s, rz1p_r.at[slot], down)

        def y_way():
            done(YB.at[slot], ry_r.at[slot])
            add_into(slot, part(0, yh, 128), YB[slot])
            send(SS.at[slot, part(zo, yh, 16)], Z2.at[slot, 0, pl.ds(0, 16)], s, rz2m_r.at[slot], up)
            send(SS.at[slot, part(zo, yh, 16, 16)], Z2.at[slot, 1, pl.ds(0, 16)], s, rz2p_r.at[slot], down)
            send(SS.at[slot, part(zn, yh, 16, 16)], Z1.at[slot, 0, pl.ds(16, 16)], s, rz1m_r.at[slot], up)
            send(SS.at[slot, part(zp_, yh, 16)], Z1.at[slot, 1, pl.ds(0, 16)], s, rz1p_r.at[slot], down)

        either(h, z_way, y_way)

    def c4(h):
        slot = rem(h, DEP)
        s = ss_s.at[slot]

        @pl.when((h >= DEP) & jnp.logical_not(y_first(h - DEP)))
        def _():
            done(YS.at[slot], ys_s.at[slot])

        def z_way():
            done(Z1.at[slot, 0], rz1m_r.at[slot])
            done(Z1.at[slot, 1], rz1p_r.at[slot])

            def total(yy):
                b = pl.ds(at16(yy * 32), 32)
                return SS[slot, part(z, yy)].astype(F32) + Z1[slot, 0, b].astype(F32) + Z1[slot, 1, b].astype(F32)

            YS[slot] = total(1 - yh).astype(BF16)
            send(YS.at[slot], YR.at[slot], ys_s.at[slot], yr_r.at[slot], across)
            TF[slot] = total(yh)

        def y_way():
            done(Z2.at[slot, 0, pl.ds(0, 16)], rz2m_r.at[slot])
            b = part(zn, yh, 16)
            add_into(slot, b, Z2[slot, 0, 0:16])
            send(SS.at[slot, b], Z1.at[slot, 0, pl.ds(0, 16)], s, rz1m_r.at[slot], up)
            done(Z2.at[slot, 1, pl.ds(0, 16)], rz2p_r.at[slot])
            b = part(zp_, yh, 16, 16)
            add_into(slot, b, Z2[slot, 1, 0:16])
            send(SS.at[slot, b], Z1.at[slot, 1, pl.ds(16, 16)], s, rz1p_r.at[slot], down)

        either(h, z_way, y_way)

    def c5(h):
        slot = rem(h, DEP)

        @pl.when(h >= DEP)
        def _():
            done(EB.at[slot, pl.ds(0, 288)], eb_s.at[slot])

        def z_way():
            done(YR.at[slot], yr_r.at[slot])
            TF[slot] += YR[slot].astype(F32)

        def y_way():
            done(Z1.at[slot, 0, pl.ds(0, 32)], rz1m_r.at[slot])
            done(Z1.at[slot, 1, pl.ds(0, 32)], rz1p_r.at[slot])
            TF[slot] = SS[slot, part(z, yh)].astype(F32) + Z1[slot, 0, 0:32].astype(F32) + Z1[slot, 1, 0:32].astype(F32)

        either(h, z_way, y_way)
        scale = jnp.where(h < NC, gslot[pl.ds(0, 32), :][:, :1], 1.0)
        EB[slot] = dot(A[...], quarters((TF[slot] * scale).astype(BF16))).astype(BF16)
        here = pl.ds(at16(x * 96), 96)
        for p, to in zip(xs, peers):
            send(EB.at[slot, pl.ds(at16(p * 96), 96)], ER.at[slot, here], eb_s.at[slot], er_r.at[slot], to)
        ER[slot, here] = EB[slot, here]

    def c6(h):
        slot = rem(h, DEP)

        @pl.when(h >= DEP)
        def _():
            done(FB.at[slot], fb_s.at[slot])

        done(ER.at[slot, pl.ds(0, 288)], er_r.at[slot])

        def total(yy):
            t = ER[slot, pl.ds(at16(yy * 48, 16), 48)].astype(F32)
            for j in range(1, 4):
                t = t + ER[slot, pl.ds(at16(96 * j + yy * 48, 16), 48)].astype(F32)
            return t

        FB[slot] = total(1 - yl).astype(BF16)
        send(FB.at[slot], FR.at[slot], fb_s.at[slot], fr_r.at[slot], pair)
        FT[slot] = total(yl)

    def c7(h):
        slot = rem(h, DEP)
        done(FR.at[slot], fr_r.at[slot])
        t = FT[slot] + FR[slot].astype(F32)
        t = jnp.concatenate([t[12 * q : 12 * q + 12] for q in range(4)], axis=1).astype(BF16)

        @pl.when(h < NC)
        def _():
            lo_ref[:, pl.ds(at16(h * CW, CW), CW)] = t

        @pl.when(h >= NC)
        def _():
            gt_ref[:, pl.ds(at16((h - NC) * CW, CW), CW)] = t

    def stage(f, i, n=2 * NC):
        @pl.when((i >= 0) & (i < n))
        def _():
            f(i)

    def step(t, carry):
        stage(a1, t + LEAD)
        stage(a2, t)
        stage(a1b, t + 1)
        stage(a3, t - LAG3)
        stage(a4, t - LAG4)
        stage(a5, t - LAG5)
        stage(ay, t - LAGY)
        stage(a6, t - LAG6)
        h = t - OFF
        stage(c7, h - L7)
        stage(c6, h - L6)
        stage(c5, h - L5)
        stage(c4, h - L4)
        stage(c3, h - L3)
        stage(c2, h - L2)
        stage(c1, h)
        return carry

    lax.fori_loop(0, STEPS, step, 0)

    def finish(g, carry):
        done(G.at[g, pl.ds(0, 336)], ge_s.at[g])
        done(R.at[g, pl.ds(0, 480)], ag_s.at[g])
        pltpu.make_async_copy(R.at[g], rg_hbm.at[g], hbm_s.at[g]).wait()
        return carry

    lax.fori_loop(0, 2 * NC, finish, 0)
    for i in range(2):
        done(SB.at[i], sb_s.at[i])
    for i in range(2 * NC - DEP, 2 * NC):
        slot = i % DEP
        if y_first(i):
            done(SS.at[slot, pl.ds(0, 224)], ss_s.at[slot])
        else:
            done(SS.at[slot, pl.ds(0, 192)], ss_s.at[slot])
            done(YS.at[slot], ys_s.at[slot])
        done(EB.at[slot, pl.ds(0, 288)], eb_s.at[slot])
        done(FB.at[slot], fb_s.at[slot])


def grads(rows, slot_grad, hid, gp, gin, gout):
    gin[...] = dot(rows[0], gp[...], ((0,), (0,))).astype(BF16)
    gout[...] = dot(hid[...], slot_grad[0], ((0,), (0,))).astype(BF16)


def local(tokens, cotangent, expert_ids, gate_values, w_in, w_out):
    vmem, hbm = pl.BlockSpec(memory_space=pltpu.VMEM), pl.BlockSpec(memory_space=pl.ANY)
    dma = lambda n: pltpu.SemaphoreType.DMA((n,))
    layer_out, grad_tokens, rg, hid, gp = pl.pallas_call(
        exchange,
        name="exchange",
        out_shape=(
            jax.ShapeDtypeStruct((12, D), BF16),
            jax.ShapeDtypeStruct((12, D), BF16),
            jax.ShapeDtypeStruct((2 * NC, ROWS, CW), BF16),
            jax.ShapeDtypeStruct((ROWS, HID), BF16),
            jax.ShapeDtypeStruct((ROWS, HID), BF16),
        ),
        in_specs=[vmem, vmem, vmem, vmem, hbm, hbm],
        out_specs=(vmem, vmem, hbm, vmem, vmem),
        scratch_shapes=[
            pltpu.VMEM((D, HID), BF16),
            pltpu.VMEM((HID, D), BF16),
            pltpu.VMEM((2 * NC, 48, QW), BF16),
            pltpu.VMEM((2 * NC, 4 * TOK, QW), BF16),
            pltpu.VMEM((2 * NC, ROWS, CW), BF16),
            pltpu.VMEM((ROWS, HID), F32),
            pltpu.VMEM((ROWS, HID), F32),
            pltpu.VMEM((4 * TOK, 128), BF16),
            pltpu.VMEM((4 * TOK, 128), F32),
            pltpu.VMEM((128, 128), F32),
            pltpu.VMEM((2, HALF, CW), BF16),
            pltpu.VMEM((HALF, CW), F32),
            pltpu.VMEM((DEP, HALF, CW), BF16),
            pltpu.VMEM((DEP, HALF, CW), BF16),
            pltpu.VMEM((DEP, 2, 32, CW), BF16),
            pltpu.VMEM((DEP, 2, 64, CW), BF16),
            pltpu.VMEM((DEP, 128, CW), BF16),
            pltpu.VMEM((DEP, 32, CW), BF16),
            pltpu.VMEM((DEP, 32, CW), BF16),
            pltpu.VMEM((DEP, 32, CW), F32),
            pltpu.VMEM((DEP, 4 * TOK, QW), BF16),
            pltpu.VMEM((DEP, 4 * TOK, QW), BF16),
            pltpu.VMEM((DEP, 48, QW), BF16),
            pltpu.VMEM((DEP, 48, QW), BF16),
            pltpu.VMEM((DEP, 48, QW), F32),
            dma(2),
        ]
        + [dma(2 * NC) for _ in range(11)]
        + [dma(2), dma(DEP), dma(DEP)]
        + [dma(DEP) for _ in range(11)],
        compiler_params=pltpu.CompilerParams(
            collective_id=0, has_side_effects=True, vmem_limit_bytes=56 * 2**20
        ),
    )(tokens, cotangent, expert_ids.T, gate_values.T, w_in[0], w_out[0])
    one = lambda f: pl.BlockSpec((1, ROWS, CW), f)
    grad_in, grad_out = pl.pallas_call(
        grads,
        name="grads",
        grid=(NC,),
        out_shape=(
            jax.ShapeDtypeStruct((D, HID), BF16),
            jax.ShapeDtypeStruct((HID, D), BF16),
        ),
        in_specs=[
            one(lambda k: (k, 0, 0)),
            one(lambda k: (NC + k, 0, 0)),
            pl.BlockSpec((ROWS, HID), lambda k: (0, 0)),
            pl.BlockSpec((ROWS, HID), lambda k: (0, 0)),
        ],
        out_specs=(
            pl.BlockSpec((CW, HID), lambda k: (k, 0)),
            pl.BlockSpec((HID, CW), lambda k: (0, k)),
        ),
        compiler_params=pltpu.CompilerParams(vmem_limit_bytes=62 * 2**20),
    )(rg, rg, hid, gp)
    return layer_out, grad_tokens, grad_in[None], grad_out[None]


def solution(mesh):
    placed = (
        P(("dp", "expert"), None),
        P(("dp", "expert"), None),
        P("dp", None),
        P("dp", None),
        P("expert", None, "dp"),
        P("expert", "dp", None),
    )
    return jax.shard_map(
        local,
        mesh=mesh,
        in_specs=placed,
        out_specs=(
            P(("dp", "expert"), None),
            P(("dp", "expert"), None),
            P("expert", None, "dp"),
            P("expert", "dp", None),
        ),
        check_vma=False,
    )
```

```python
import functools
import jax
import jax.numpy as jnp
from jax import lax
from jax.experimental import pallas as pl
from jax.experimental.pallas import tpu as pltpu
from jax.sharding import PartitionSpec as P

D = 6144
HID = 512
CAP = 32
TOK = 96
NC = 6
CW = D // NC
QW = CW // 4
ROWS = 512
HALF = 256
DEP = 6
MOD, WHICH = 3, 2
LEAD = 3
LAG3, LAG4, LAG5, LAGY, LAG6 = 1, 3, 5, 6, 7
OFF = NC + LAG6
L2, L3, L4, L5, L6, L7 = 1, 3, 5, 7, 9, 11
STEPS = OFF + 2 * NC + L7
MESH = pl.DeviceIdType.MESH
F32, BF16 = jnp.float32, jnp.bfloat16


def rem(a, b):
    return lax.rem(a, jnp.int32(b))


def at16(v, m=32):
    return pl.multiple_of(v, m)


def dot(a, b, dims=((1,), (0,)), precision=None):
    return lax.dot_general(a, b, (dims, ((), ())), precision=precision, preferred_element_type=F32)


def y_first(i):
    return i % MOD == WHICH if isinstance(i, int) else rem(i, MOD) == WHICH


def done(ref, sem):
    pltpu.make_async_copy(ref, ref, sem).wait()


def exchange(
    tok_ref, cot_ref, ids_ref, gates_ref, win_hbm, wout_hbm,
    lo_ref, gt_ref, rt_hbm, sg_hbm, hidt, gp,
    win, wout, X, G, R, RT, hid, pre, gh, A, AT, grep, gslot,
    SB, PO, RB, SS, Z2, Z1, YB, YS, YR, TF, EB, ER, FB, FR, FT,
    w_sem, ge_s, ge_r, gp_r, ag_s, y_r, zm_r, zp_r, z2m_r, z2p_r, sib_r, hbm_s,
    sb_s, rb_r, ss_s, ry_r, rz2m_r, rz2p_r, rz1m_r, rz1p_r, ys_s, yr_r, eb_s, er_r, fb_s, fr_r,
):
    dp, e = lax.axis_index("dp"), lax.axis_index("expert")
    z, yh, c = dp // 4, (dp // 2) % 2, dp % 2
    yl, x = e // 4, e % 4

    def at(zz, yy, cc):
        return (zz * 4 + yy * 2 + cc, e)

    zn, zp_, zo = rem(z + 1, 4), rem(z + 3, 4), rem(z + 2, 4)
    up, down, across, sib = at(zn, yh, c), at(zp_, yh, c), at(z, 1 - yh, c), at(z, yh, 1 - c)
    xs = [rem(x + d, 4) for d in range(1, 4)]
    peers = [(dp, yl * 4 + p) for p in xs]
    far = [(dp, (1 - yl) * 4 + p) for p in xs]
    pair = (dp, (1 - yl) * 4 + x)

    def send(src, dst, ss, rs, to):
        pltpu.make_async_remote_copy(
            src_ref=src, dst_ref=dst, send_sem=ss, recv_sem=rs, device_id=to, device_id_type=MESH
        ).start()

    load_in = pltpu.make_async_copy(win_hbm, win, w_sem.at[0])
    load_out = pltpu.make_async_copy(wout_hbm, wout, w_sem.at[1])
    load_in.start()
    load_out.start()

    barrier = pltpu.get_barrier_semaphore()
    for to in [up, down, across, sib, pair] + peers + far:
        pl.semaphore_signal(barrier, inc=1, device_id=to, device_id_type=MESH)
    pl.semaphore_wait(barrier, 11)

    mine = pl.ds(at16((x * 2 + yl) * 48, 16), 48)
    twin = pl.ds(at16((x * 2 + 1 - yl) * 48, 16), 48)

    def quarters(v):
        return jnp.concatenate([v[:, q * QW : (q + 1) * QW] for q in range(4)], axis=0)

    def a1(g, reach=()):
        k = jnp.where(g < NC, g, g - NC)
        where = pl.ds(at16(k * CW, CW), CW)
        v = jnp.where(g < NC, tok_ref[:, where].astype(F32), cot_ref[:, where].astype(F32))
        v = quarters(v).astype(BF16)
        X[g] = v
        G[g, mine] = v
        send(X.at[g], G.at[g, mine], ge_s.at[g], gp_r.at[g], pair)
        for to in [*peers, *reach]:
            send(X.at[g], G.at[g, mine], ge_s.at[g], ge_r.at[g], to)

    def a1b(g):
        b = G.at[g, twin]
        done(b, gp_r.at[g])
        for to in peers:
            send(b, b, ge_s.at[g], ge_r.at[g], to)

    a1(jnp.int32(0), far)
    for g in range(1, LEAD):
        a1(jnp.int32(g))

    chosen = ids_ref[...] == e
    gsum = jnp.sum(jnp.where(chosen, gates_ref[...], 0.0), axis=0, keepdims=True)
    picked = jnp.max(jnp.where(chosen, 1.0, 0.0), axis=0, keepdims=True)
    row = lax.broadcasted_iota(jnp.int32, (TOK, TOK), 0)
    col = lax.broadcasted_iota(jnp.int32, (TOK, TOK), 1)
    tri = jnp.where(row <= col, 1.0, 0.0).astype(BF16)
    pickb = jnp.broadcast_to(picked, (128, TOK))
    place = dot(pickb.astype(BF16), tri) - 1.0
    slots = jnp.bitwise_and(lax.broadcasted_iota(jnp.int32, (128, TOK), 0), 31).astype(F32)
    table = jnp.where(place == slots, pickb, 0.0)
    r4 = lax.broadcasted_iota(jnp.int32, (4 * TOK, 128), 0)
    c4_ = lax.broadcasted_iota(jnp.int32, (4 * TOK, 128), 1)
    j4 = jnp.right_shift(r4 * 683, 15)
    rest = r4 - j4 * 48
    q_r = jnp.right_shift(rest * 171, 11)
    token = (jnp.bitwise_and(j4, 1) * 4 + jnp.right_shift(j4, 1)) * 12 + rest - q_r * 12
    q_c = jnp.right_shift(c4_, 5)
    widen = jnp.where(token == c4_, 1.0, 0.0)[:, :TOK]
    nt = ((1,), (1,))
    wide = dot(widen.astype(BF16), table.astype(BF16), nt)
    wide = jnp.where(q_r == q_c, wide, 0.0)
    A[...] = wide.astype(BF16)
    AT[...] = wide.T.astype(BF16)
    gsb = jnp.broadcast_to(gsum, (128, TOK))
    grep[...] = dot(widen, gsb, nt, lax.Precision.HIGHEST)
    gslot[...] = dot(table, gsb, nt, lax.Precision.HIGHEST)

    done(G.at[0, twin], gp_r.at[0])
    a1b(jnp.int32(1))

    pre[...] = jnp.zeros_like(pre)
    gh[...] = jnp.zeros_like(gh)

    def block(zz, yy, n=32, skip=0):
        return pl.ds(at16((c * 8 + yy * 4 + zz) * 32 + skip, 16), n)

    def to_sib(g, where):
        send(R.at[g, where], R.at[g, where], ag_s.at[g], sib_r.at[g], sib)

    def a2(g):
        done(G.at[g, pl.ds(0, 288)], ge_r.at[g])
        scale = jnp.where(g < NC, 1.0, grep[...][:, :1])
        v = (G[g].astype(F32) * scale).astype(BF16)
        packed = dot(AT[...], v).astype(BF16)
        own = block(z, yh)
        for q in range(4):
            R[g, own, q * QW : (q + 1) * QW] = packed[q * 32 : (q + 1) * 32]
        me = R.at[g, own]
        send(me, me, ag_s.at[g], y_r.at[g], across)
        send(me, me, ag_s.at[g], zm_r.at[g], up)
        send(me, me, ag_s.at[g], zp_r.at[g], down)
        to_sib(g, own)

    def a3(g):
        @pl.when(jnp.logical_not(y_first(g)))
        def _():
            theirs = block(z, 1 - yh)
            b = R.at[g, theirs]
            done(b, y_r.at[g])
            send(b, b, ag_s.at[g], zm_r.at[g], up)
            send(b, b, ag_s.at[g], zp_r.at[g], down)
            to_sib(g, theirs)

    def a4(g):
        def hand_on(zz, sem, sem2, to, pick):
            @pl.when(jnp.logical_not(y_first(g)))
            def _():
                done(R.at[g, pl.ds(0, 64)], sem.at[g])
                b = R.at[g, block(zz, pick)]
                send(b, b, ag_s.at[g], sem2.at[g], to)
                to_sib(g, block(zz, 0))
                to_sib(g, block(zz, 1))

            @pl.when(y_first(g))
            def _():
                whole = R.at[g, block(zz, yh)]
                done(whole, sem.at[g])
                b = R.at[g, block(zz, yh, 16, 16 * pick)]
                send(b, b, ag_s.at[g], sem2.at[g], to)
                send(whole, whole, ag_s.at[g], y_r.at[g], across)
                to_sib(g, block(zz, yh))

        hand_on(zp_, zm_r, z2m_r, up, 0)
        hand_on(zn, zp_r, z2p_r, down, 1)

    def a5(g):
        @pl.when(jnp.logical_not(y_first(g)))
        def _():
            done(R.at[g, block(zo, 0)], z2m_r.at[g])
            done(R.at[g, block(zo, 1)], z2p_r.at[g])
            to_sib(g, block(zo, 0))
            to_sib(g, block(zo, 1))

        @pl.when(y_first(g))
        def _():
            done(R.at[g, block(zo, yh, 16)], z2m_r.at[g])
            done(R.at[g, block(zo, yh, 16, 16)], z2p_r.at[g])
            b = R.at[g, block(zo, yh)]
            send(b, b, ag_s.at[g], y_r.at[g], across)
            to_sib(g, block(zo, yh))

    def ay(g):
        @pl.when(y_first(g))
        def _():
            b = block(0, 1 - yh, 128)
            done(R.at[g, b], y_r.at[g])
            to_sib(g, b)

    def a6(g):
        done(R.at[g, pl.ds(at16((1 - c) * HALF), HALF)], sib_r.at[g])

        @pl.when(g == 0)
        def _():
            load_in.wait()
            load_out.wait()

        @pl.when(g < NC)
        def _():
            where = pl.ds(at16(g * CW, CW), CW)
            pre[...] += dot(R[g], win[where, :])
            RT[where, :] = R[g].T
            pltpu.make_async_copy(RT.at[where], rt_hbm.at[where], hbm_s.at[g]).start()

        @pl.when(g >= NC)
        def _():
            pltpu.make_async_copy(R.at[g], sg_hbm.at[g - NC], hbm_s.at[g]).start()
            gh[...] += dot(R[g], wout[:, pl.ds(at16((g - NC) * CW, CW), CW)], ((1,), (1,)))

        @pl.when(g == NC - 1)
        def _():
            v = pre[...]
            v = v * jax.nn.sigmoid(v)
            hid[...] = v.astype(BF16)
            hidt[...] = v.T.astype(BF16)

        @pl.when(g == 2 * NC - 1)
        def _():
            v = pre[...]
            s = jax.nn.sigmoid(v)
            gp[...] = (gh[...] * s * (1.0 + v * (1.0 - s))).astype(BF16)

    ours, others = pl.ds(at16(c * HALF), HALF), pl.ds(at16((1 - c) * HALF), HALF)

    def c1(h):
        two, slot = rem(h, 2), rem(h, DEP)

        @pl.when(h >= 2)
        def _():
            done(SB.at[two], sb_s.at[two])

        def product(lhs, w, dims):
            SB[two] = dot(lhs[others, :], w, dims).astype(BF16)
            send(SB.at[two], RB.at[slot], sb_s.at[two], rb_r.at[slot], sib)
            PO[...] = dot(lhs[ours, :], w, dims)

        @pl.when(h < NC)
        def _():
            product(hid, wout[:, pl.ds(at16(h * CW, CW), CW)], ((1,), (0,)))

        @pl.when(h >= NC)
        def _():
            product(gp, win[pl.ds(at16((h - NC) * CW, CW), CW), :], ((1,), (1,)))

    def part(zz, yy, n=32, skip=0):
        return pl.ds(at16((yy * 4 + zz) * 32 + skip, 16), n)

    def either(h, z_way, y_way):
        pl.when(jnp.logical_not(y_first(h)))(z_way)
        pl.when(y_first(h))(y_way)

    def sent(slot, i):
        either(
            i,
            lambda: done(SS.at[slot, pl.ds(0, 192)], ss_s.at[slot]),
            lambda: done(SS.at[slot, pl.ds(0, 224)], ss_s.at[slot]),
        )

    def add_into(slot, b, v):
        SS[slot, b] = (SS[slot, b].astype(F32) + v.astype(F32)).astype(BF16)

    def c2(h):
        slot = rem(h, DEP)

        @pl.when(h >= DEP)
        def _():
            sent(slot, h - DEP)

        done(RB.at[slot], rb_r.at[slot])
        SS[slot] = (PO[...] + RB[slot].astype(F32)).astype(BF16)
        s = ss_s.at[slot]

        def z_way():
            send(SS.at[slot, part(zo, 0)], Z2.at[slot, 0], s, rz2m_r.at[slot], up)
            send(SS.at[slot, part(zo, 1)], Z2.at[slot, 1], s, rz2p_r.at[slot], down)
            send(SS.at[slot, part(zn, 1)], Z1.at[slot, 0, pl.ds(32, 32)], s, rz1m_r.at[slot], up)
            send(SS.at[slot, part(zp_, 0)], Z1.at[slot, 1, pl.ds(0, 32)], s, rz1p_r.at[slot], down)

        def y_way():
            send(SS.at[slot, part(0, 1 - yh, 128)], YB.at[slot], s, ry_r.at[slot], across)

        either(h, z_way, y_way)

    def c3(h):
        slot = rem(h, DEP)
        s = ss_s.at[slot]

        def z_way():
            done(Z2.at[slot, 0], rz2m_r.at[slot])
            b = part(zn, 0)
            add_into(slot, b, Z2[slot, 0])
            send(SS.at[slot, b], Z1.at[slot, 0, pl.ds(0, 32)], s, rz1m_r.at[slot], up)
            done(Z2.at[slot, 1], rz2p_r.at[slot])
            b = part(zp_, 1)
            add_into(slot, b, Z2[slot, 1])
            send(SS.at[slot, b], Z1.at[slot, 1, pl.ds(32, 32)], s, rz1p_r.at[slot], down)

        def y_way():
            done(YB.at[slot], ry_r.at[slot])
            add_into(slot, part(0, yh, 128), YB[slot])
            send(SS.at[slot, part(zo, yh, 16)], Z2.at[slot, 0, pl.ds(0, 16)], s, rz2m_r.at[slot], up)
            send(SS.at[slot, part(zo, yh, 16, 16)], Z2.at[slot, 1, pl.ds(0, 16)], s, rz2p_r.at[slot], down)
            send(SS.at[slot, part(zn, yh, 16, 16)], Z1.at[slot, 0, pl.ds(16, 16)], s, rz1m_r.at[slot], up)
            send(SS.at[slot, part(zp_, yh, 16)], Z1.at[slot, 1, pl.ds(0, 16)], s, rz1p_r.at[slot], down)

        either(h, z_way, y_way)

    def c4(h):
        slot = rem(h, DEP)
        s = ss_s.at[slot]

        @pl.when((h >= DEP) & jnp.logical_not(y_first(h - DEP)))
        def _():
            done(YS.at[slot], ys_s.at[slot])

        def z_way():
            done(Z1.at[slot, 0], rz1m_r.at[slot])
            done(Z1.at[slot, 1], rz1p_r.at[slot])

            def total(yy):
                b = pl.ds(at16(yy * 32), 32)
                return SS[slot, part(z, yy)].astype(F32) + Z1[slot, 0, b].astype(F32) + Z1[slot, 1, b].astype(F32)

            YS[slot] = total(1 - yh).astype(BF16)
            send(YS.at[slot], YR.at[slot], ys_s.at[slot], yr_r.at[slot], across)
            TF[slot] = total(yh)

        def y_way():
            done(Z2.at[slot, 0, pl.ds(0, 16)], rz2m_r.at[slot])
            b = part(zn, yh, 16)
            add_into(slot, b, Z2[slot, 0, 0:16])
            send(SS.at[slot, b], Z1.at[slot, 0, pl.ds(0, 16)], s, rz1m_r.at[slot], up)
            done(Z2.at[slot, 1, pl.ds(0, 16)], rz2p_r.at[slot])
            b = part(zp_, yh, 16, 16)
            add_into(slot, b, Z2[slot, 1, 0:16])
            send(SS.at[slot, b], Z1.at[slot, 1, pl.ds(16, 16)], s, rz1p_r.at[slot], down)

        either(h, z_way, y_way)

    def c5(h):
        slot = rem(h, DEP)

        @pl.when(h >= DEP)
        def _():
            done(EB.at[slot, pl.ds(0, 288)], eb_s.at[slot])

        def z_way():
            done(YR.at[slot], yr_r.at[slot])
            TF[slot] += YR[slot].astype(F32)

        def y_way():
            done(Z1.at[slot, 0, pl.ds(0, 32)], rz1m_r.at[slot])
            done(Z1.at[slot, 1, pl.ds(0, 32)], rz1p_r.at[slot])
            TF[slot] = SS[slot, part(z, yh)].astype(F32) + Z1[slot, 0, 0:32].astype(F32) + Z1[slot, 1, 0:32].astype(F32)

        either(h, z_way, y_way)
        scale = jnp.where(h < NC, gslot[pl.ds(0, 32), :][:, :1], 1.0)
        EB[slot] = dot(A[...], quarters((TF[slot] * scale).astype(BF16))).astype(BF16)
        here = pl.ds(at16(x * 96), 96)
        for p, to in zip(xs, peers):
            send(EB.at[slot, pl.ds(at16(p * 96), 96)], ER.at[slot, here], eb_s.at[slot], er_r.at[slot], to)
        ER[slot, here] = EB[slot, here]

    def c6(h):
        slot = rem(h, DEP)

        @pl.when(h >= DEP)
        def _():
            done(FB.at[slot], fb_s.at[slot])

        done(ER.at[slot, pl.ds(0, 288)], er_r.at[slot])

        def total(yy):
            t = ER[slot, pl.ds(at16(yy * 48, 16), 48)].astype(F32)
            for j in range(1, 4):
                t = t + ER[slot, pl.ds(at16(96 * j + yy * 48, 16), 48)].astype(F32)
            return t

        FB[slot] = total(1 - yl).astype(BF16)
        send(FB.at[slot], FR.at[slot], fb_s.at[slot], fr_r.at[slot], pair)
        FT[slot] = total(yl)

    def c7(h):
        slot = rem(h, DEP)
        done(FR.at[slot], fr_r.at[slot])
        t = FT[slot] + FR[slot].astype(F32)
        t = jnp.concatenate([t[12 * q : 12 * q + 12] for q in range(4)], axis=1).astype(BF16)

        @pl.when(h < NC)
        def _():
            lo_ref[:, pl.ds(at16(h * CW, CW), CW)] = t

        @pl.when(h >= NC)
        def _():
            gt_ref[:, pl.ds(at16((h - NC) * CW, CW), CW)] = t

    def stage(f, i, n=2 * NC):
        @pl.when((i >= 0) & (i < n))
        def _():
            f(i)

    def step(t, carry):
        stage(a1, t + LEAD)
        stage(a2, t)
        stage(a1b, t + 2)
        stage(a3, t - LAG3)
        stage(a4, t - LAG4)
        stage(a5, t - LAG5)
        stage(ay, t - LAGY)
        stage(a6, t - LAG6)
        h = t - OFF
        stage(c7, h - L7)
        stage(c6, h - L6)
        stage(c5, h - L5)
        stage(c4, h - L4)
        stage(c3, h - L3)
        stage(c2, h - L2)
        stage(c1, h)
        return carry

    lax.fori_loop(0, STEPS, step, 0)

    def finish(g, carry):
        done(G.at[g, pl.ds(0, 336)], ge_s.at[g])
        done(R.at[g, pl.ds(0, 480)], ag_s.at[g])
        done(R.at[g], hbm_s.at[g])
        return carry

    lax.fori_loop(0, 2 * NC, finish, 0)
    for i in range(2):
        done(SB.at[i], sb_s.at[i])
    for i in range(2 * NC - DEP, 2 * NC):
        slot = i % DEP
        if y_first(i):
            done(SS.at[slot, pl.ds(0, 224)], ss_s.at[slot])
        else:
            done(SS.at[slot, pl.ds(0, 192)], ss_s.at[slot])
            done(YS.at[slot], ys_s.at[slot])
        done(EB.at[slot, pl.ds(0, 288)], eb_s.at[slot])
        done(FB.at[slot], fb_s.at[slot])


def grads(rows_t, slot_grad, hid_t, gp, gin, gout):
    gin[...] = dot(rows_t[...], gp[...]).astype(BF16)
    gout[...] = dot(hid_t[...], slot_grad[0]).astype(BF16)


def local(tokens, cotangent, expert_ids, gate_values, w_in, w_out):
    vmem, hbm = pl.BlockSpec(memory_space=pltpu.VMEM), pl.BlockSpec(memory_space=pl.ANY)
    dma = lambda n: pltpu.SemaphoreType.DMA((n,))
    layer_out, grad_tokens, rows_t, slot_grad, hid_t, gp = pl.pallas_call(
        exchange,
        name="exchange",
        out_shape=(
            jax.ShapeDtypeStruct((12, D), BF16),
            jax.ShapeDtypeStruct((12, D), BF16),
            jax.ShapeDtypeStruct((D, ROWS), BF16),
            jax.ShapeDtypeStruct((NC, ROWS, CW), BF16),
            jax.ShapeDtypeStruct((ROWS, HID), BF16),
            jax.ShapeDtypeStruct((ROWS, HID), BF16),
        ),
        in_specs=[vmem, vmem, vmem, vmem, hbm, hbm],
        out_specs=(vmem, vmem, hbm, hbm, vmem, vmem),
        scratch_shapes=[
            pltpu.VMEM((D, HID), BF16),
            pltpu.VMEM((HID, D), BF16),
            pltpu.VMEM((2 * NC, 48, QW), BF16),
            pltpu.VMEM((2 * NC, 4 * TOK, QW), BF16),
            pltpu.VMEM((2 * NC, ROWS, CW), BF16),
            pltpu.VMEM((D, ROWS), BF16),
            pltpu.VMEM((ROWS, HID), BF16),
            pltpu.VMEM((ROWS, HID), F32),
            pltpu.VMEM((ROWS, HID), F32),
            pltpu.VMEM((4 * TOK, 128), BF16),
            pltpu.VMEM((128, 4 * TOK), BF16),
            pltpu.VMEM((4 * TOK, 128), F32),
            pltpu.VMEM((128, 128), F32),
            pltpu.VMEM((2, HALF, CW), BF16),
            pltpu.VMEM((HALF, CW), F32),
            pltpu.VMEM((DEP, HALF, CW), BF16),
            pltpu.VMEM((DEP, HALF, CW), BF16),
            pltpu.VMEM((DEP, 2, 32, CW), BF16),
            pltpu.VMEM((DEP, 2, 64, CW), BF16),
            pltpu.VMEM((DEP, 128, CW), BF16),
            pltpu.VMEM((DEP, 32, CW), BF16),
            pltpu.VMEM((DEP, 32, CW), BF16),
            pltpu.VMEM((DEP, 32, CW), F32),
            pltpu.VMEM((DEP, 4 * TOK, QW), BF16),
            pltpu.VMEM((DEP, 4 * TOK, QW), BF16),
            pltpu.VMEM((DEP, 48, QW), BF16),
            pltpu.VMEM((DEP, 48, QW), BF16),
            pltpu.VMEM((DEP, 48, QW), F32),
            dma(2),
        ]
        + [dma(2 * NC) for _ in range(11)]
        + [dma(2), dma(DEP), dma(DEP)]
        + [dma(DEP) for _ in range(11)],
        compiler_params=pltpu.CompilerParams(
            collective_id=0, has_side_effects=True, vmem_limit_bytes=56 * 2**20
        ),
    )(tokens, cotangent, expert_ids.T, gate_values.T, w_in[0], w_out[0])
    grad_in, grad_out = pl.pallas_call(
        grads,
        name="grads",
        grid=(NC,),
        out_shape=(
            jax.ShapeDtypeStruct((D, HID), BF16),
            jax.ShapeDtypeStruct((HID, D), BF16),
        ),
        in_specs=[
            pl.BlockSpec((CW, ROWS), lambda k: (k, 0)),
            pl.BlockSpec((1, ROWS, CW), lambda k: (k, 0, 0)),
            pl.BlockSpec((ROWS, HID), lambda k: (0, 0)),
            pl.BlockSpec((ROWS, HID), lambda k: (0, 0)),
        ],
        out_specs=(
            pl.BlockSpec((CW, HID), lambda k: (k, 0)),
            pl.BlockSpec((HID, CW), lambda k: (0, k)),
        ),
        compiler_params=pltpu.CompilerParams(vmem_limit_bytes=62 * 2**20),
    )(rows_t, slot_grad, hid_t, gp)
    return layer_out, grad_tokens, grad_in[None], grad_out[None]


def solution(mesh):
    placed = (
        P(("dp", "expert"), None),
        P(("dp", "expert"), None),
        P("dp", None),
        P("dp", None),
        P("expert", None, "dp"),
        P("expert", "dp", None),
    )
    return jax.shard_map(
        local,
        mesh=mesh,
        in_specs=placed,
        out_specs=(
            P(("dp", "expert"), None),
            P(("dp", "expert"), None),
            P("expert", None, "dp"),
            P("expert", "dp", None),
        ),
        check_vma=False,
    )
```

```python
import functools
import jax
import jax.numpy as jnp
from jax import lax
from jax.experimental import pallas as pl
from jax.experimental.pallas import tpu as pltpu
from jax.sharding import PartitionSpec as P

D = 6144
HID = 512
CAP = 32
TOK = 96
NC = 6
CW = D // NC
QW = CW // 4
ROWS = 512
HALF = 256
DEP = 6
MOD, WHICH = 3, 0
LEAD = 3
LAG3, LAG4, LAG5, LAGY, LAG6 = 1, 3, 5, 6, 7
OFF = NC + LAG6
L2, L3, L4, L5, L6, L7 = 1, 3, 5, 7, 10, 13
STEPS = OFF + 2 * NC + L7
MESH = pl.DeviceIdType.MESH
F32, BF16 = jnp.float32, jnp.bfloat16


def rem(a, b):
    return lax.rem(a, jnp.int32(b))


def at16(v, m=32):
    return pl.multiple_of(v, m)


def dot(a, b, dims=((1,), (0,)), precision=None):
    return lax.dot_general(a, b, (dims, ((), ())), precision=precision, preferred_element_type=F32)


def y_first(i):
    return i % MOD == WHICH if isinstance(i, int) else rem(i, MOD) == WHICH


def done(ref, sem):
    pltpu.make_async_copy(ref, ref, sem).wait()


def exchange(
    tok_ref, cot_ref, ids_ref, gates_ref, win_hbm, wout_hbm,
    lo_ref, gt_ref, rt_hbm, sg_hbm, hidt, gp,
    win, wout, X, G, R, RT, hid, pre, gh, A, AT, grep, gslot,
    SB, PO, RB, SS, Z2, Z1, YB, YS, YR, TF, EB, ER, FB, FR, FT,
    w_sem, ge_s, ge_r, gp_r, ag_s, y_r, zm_r, zp_r, z2m_r, z2p_r, sib_r, hbm_s,
    sb_s, rb_r, ss_s, ry_r, rz2m_r, rz2p_r, rz1m_r, rz1p_r, ys_s, yr_r, eb_s, er_r, fb_s, fr_r,
):
    dp, e = lax.axis_index("dp"), lax.axis_index("expert")
    z, yh, c = dp // 4, (dp // 2) % 2, dp % 2
    yl, x = e // 4, e % 4

    def at(zz, yy, cc):
        return (zz * 4 + yy * 2 + cc, e)

    zn, zp_, zo = rem(z + 1, 4), rem(z + 3, 4), rem(z + 2, 4)
    up, down, across, sib = at(zn, yh, c), at(zp_, yh, c), at(z, 1 - yh, c), at(z, yh, 1 - c)
    xs = [rem(x + d, 4) for d in range(1, 4)]
    peers = [(dp, yl * 4 + p) for p in xs]
    far = [(dp, (1 - yl) * 4 + p) for p in xs]
    pair = (dp, (1 - yl) * 4 + x)

    def send(src, dst, ss, rs, to):
        pltpu.make_async_remote_copy(
            src_ref=src, dst_ref=dst, send_sem=ss, recv_sem=rs, device_id=to, device_id_type=MESH
        ).start()

    load_in = pltpu.make_async_copy(win_hbm, win, w_sem.at[0])
    load_out = pltpu.make_async_copy(wout_hbm, wout, w_sem.at[1])
    load_in.start()
    load_out.start()

    barrier = pltpu.get_barrier_semaphore()
    for to in [up, down, across, sib, pair] + peers + far:
        pl.semaphore_signal(barrier, inc=1, device_id=to, device_id_type=MESH)
    pl.semaphore_wait(barrier, 11)

    mine = pl.ds(at16((x * 2 + yl) * 48, 16), 48)
    twin = pl.ds(at16((x * 2 + 1 - yl) * 48, 16), 48)

    def quarters(v):
        return jnp.concatenate([v[:, q * QW : (q + 1) * QW] for q in range(4)], axis=0)

    def a1(g, reach=()):
        k = jnp.where(g < NC, g, g - NC)
        where = pl.ds(at16(k * CW, CW), CW)
        v = jnp.where(g < NC, tok_ref[:, where].astype(F32), cot_ref[:, where].astype(F32))
        v = quarters(v).astype(BF16)
        X[g] = v
        G[g, mine] = v
        send(X.at[g], G.at[g, mine], ge_s.at[g], gp_r.at[g], pair)
        for to in [*peers, *reach]:
            send(X.at[g], G.at[g, mine], ge_s.at[g], ge_r.at[g], to)

    def a1b(g):
        b = G.at[g, twin]
        done(b, gp_r.at[g])
        for to in peers:
            send(b, b, ge_s.at[g], ge_r.at[g], to)

    a1(jnp.int32(0), far)
    for g in range(1, LEAD):
        a1(jnp.int32(g))

    chosen = ids_ref[...] == e
    gsum = jnp.sum(jnp.where(chosen, gates_ref[...], 0.0), axis=0, keepdims=True)
    picked = jnp.max(jnp.where(chosen, 1.0, 0.0), axis=0, keepdims=True)
    row = lax.broadcasted_iota(jnp.int32, (TOK, TOK), 0)
    col = lax.broadcasted_iota(jnp.int32, (TOK, TOK), 1)
    tri = jnp.where(row <= col, 1.0, 0.0).astype(BF16)
    pickb = jnp.broadcast_to(picked, (128, TOK))
    place = dot(pickb.astype(BF16), tri) - 1.0
    slots = jnp.bitwise_and(lax.broadcasted_iota(jnp.int32, (128, TOK), 0), 31).astype(F32)
    table = jnp.where(place == slots, pickb, 0.0)
    r4 = lax.broadcasted_iota(jnp.int32, (4 * TOK, 128), 0)
    c4_ = lax.broadcasted_iota(jnp.int32, (4 * TOK, 128), 1)
    j4 = jnp.right_shift(r4 * 683, 15)
    rest = r4 - j4 * 48
    q_r = jnp.right_shift(rest * 171, 11)
    token = (jnp.bitwise_and(j4, 1) * 4 + jnp.right_shift(j4, 1)) * 12 + rest - q_r * 12
    q_c = jnp.right_shift(c4_, 5)
    widen = jnp.where(token == c4_, 1.0, 0.0)[:, :TOK]
    nt = ((1,), (1,))
    wide = dot(widen.astype(BF16), table.astype(BF16), nt)
    wide = jnp.where(q_r == q_c, wide, 0.0)
    A[...] = wide.astype(BF16)
    AT[...] = wide.T.astype(BF16)
    gsb = jnp.broadcast_to(gsum, (128, TOK))
    grep[...] = dot(widen, gsb, nt, lax.Precision.HIGHEST)
    gslot[...] = dot(table, gsb, nt, lax.Precision.HIGHEST)

    done(G.at[0, twin], gp_r.at[0])
    a1b(jnp.int32(1))

    pre[...] = jnp.zeros_like(pre)
    gh[...] = jnp.zeros_like(gh)

    def block(zz, yy, n=32, skip=0):
        return pl.ds(at16((c * 8 + yy * 4 + zz) * 32 + skip, 16), n)

    def to_sib(g, where):
        send(R.at[g, where], R.at[g, where], ag_s.at[g], sib_r.at[g], sib)

    def a2(g):
        done(G.at[g, pl.ds(0, 288)], ge_r.at[g])
        scale = jnp.where(g < NC, 1.0, grep[...][:, :1])
        v = (G[g].astype(F32) * scale).astype(BF16)
        packed = dot(AT[...], v).astype(BF16)
        own = block(z, yh)
        for q in range(4):
            R[g, own, q * QW : (q + 1) * QW] = packed[q * 32 : (q + 1) * 32]
        me = R.at[g, own]
        send(me, me, ag_s.at[g], y_r.at[g], across)
        send(me, me, ag_s.at[g], zm_r.at[g], up)
        send(me, me, ag_s.at[g], zp_r.at[g], down)
        to_sib(g, own)

    def a3(g):
        @pl.when(jnp.logical_not(y_first(g)))
        def _():
            theirs = block(z, 1 - yh)
            b = R.at[g, theirs]
            done(b, y_r.at[g])
            send(b, b, ag_s.at[g], zm_r.at[g], up)
            send(b, b, ag_s.at[g], zp_r.at[g], down)
            to_sib(g, theirs)

    def a4(g):
        def hand_on(zz, sem, sem2, to, pick):
            @pl.when(jnp.logical_not(y_first(g)))
            def _():
                done(R.at[g, pl.ds(0, 64)], sem.at[g])
                b = R.at[g, block(zz, pick)]
                send(b, b, ag_s.at[g], sem2.at[g], to)
                to_sib(g, block(zz, 0))
                to_sib(g, block(zz, 1))

            @pl.when(y_first(g))
            def _():
                whole = R.at[g, block(zz, yh)]
                done(whole, sem.at[g])
                b = R.at[g, block(zz, yh, 16, 16 * pick)]
                send(b, b, ag_s.at[g], sem2.at[g], to)
                send(whole, whole, ag_s.at[g], y_r.at[g], across)
                to_sib(g, block(zz, yh))

        hand_on(zp_, zm_r, z2m_r, up, 0)
        hand_on(zn, zp_r, z2p_r, down, 1)

    def a5(g):
        @pl.when(jnp.logical_not(y_first(g)))
        def _():
            done(R.at[g, block(zo, 0)], z2m_r.at[g])
            done(R.at[g, block(zo, 1)], z2p_r.at[g])
            to_sib(g, block(zo, 0))
            to_sib(g, block(zo, 1))

        @pl.when(y_first(g))
        def _():
            done(R.at[g, block(zo, yh, 16)], z2m_r.at[g])
            done(R.at[g, block(zo, yh, 16, 16)], z2p_r.at[g])
            b = R.at[g, block(zo, yh)]
            send(b, b, ag_s.at[g], y_r.at[g], across)
            to_sib(g, block(zo, yh))

    def ay(g):
        @pl.when(y_first(g))
        def _():
            b = block(0, 1 - yh, 128)
            done(R.at[g, b], y_r.at[g])
            to_sib(g, b)

    def a6(g):
        done(R.at[g, pl.ds(at16((1 - c) * HALF), HALF)], sib_r.at[g])

        @pl.when(g == 0)
        def _():
            load_in.wait()
            load_out.wait()

        @pl.when(g < NC)
        def _():
            where = pl.ds(at16(g * CW, CW), CW)
            pre[...] += dot(R[g], win[where, :])
            RT[where, :] = R[g].T
            pltpu.make_async_copy(RT.at[where], rt_hbm.at[where], hbm_s.at[g]).start()

        @pl.when(g >= NC)
        def _():
            pltpu.make_async_copy(R.at[g], sg_hbm.at[g - NC], hbm_s.at[g]).start()
            gh[...] += dot(R[g], wout[:, pl.ds(at16((g - NC) * CW, CW), CW)], ((1,), (1,)))

        @pl.when(g == NC - 1)
        def _():
            v = pre[...]
            v = v * jax.nn.sigmoid(v)
            hid[...] = v.astype(BF16)
            hidt[...] = v.T.astype(BF16)

        @pl.when(g == 2 * NC - 1)
        def _():
            v = pre[...]
            s = jax.nn.sigmoid(v)
            gp[...] = (gh[...] * s * (1.0 + v * (1.0 - s))).astype(BF16)

    ours, others = pl.ds(at16(c * HALF), HALF), pl.ds(at16((1 - c) * HALF), HALF)

    def c1(h):
        two, slot = rem(h, 2), rem(h, DEP)

        @pl.when(h >= 2)
        def _():
            done(SB.at[two], sb_s.at[two])

        def product(lhs, w, dims):
            SB[two] = dot(lhs[others, :], w, dims).astype(BF16)
            send(SB.at[two], RB.at[slot], sb_s.at[two], rb_r.at[slot], sib)
            PO[...] = dot(lhs[ours, :], w, dims)

        @pl.when(h < NC)
        def _():
            product(hid, wout[:, pl.ds(at16(h * CW, CW), CW)], ((1,), (0,)))

        @pl.when(h >= NC)
        def _():
            product(gp, win[pl.ds(at16((h - NC) * CW, CW), CW), :], ((1,), (1,)))

    def part(zz, yy, n=32, skip=0):
        return pl.ds(at16((yy * 4 + zz) * 32 + skip, 16), n)

    def either(h, z_way, y_way):
        pl.when(jnp.logical_not(y_first(h)))(z_way)
        pl.when(y_first(h))(y_way)

    def sent(slot, i):
        either(
            i,
            lambda: done(SS.at[slot, pl.ds(0, 192)], ss_s.at[slot]),
            lambda: done(SS.at[slot, pl.ds(0, 224)], ss_s.at[slot]),
        )

    def add_into(slot, b, v):
        SS[slot, b] = (SS[slot, b].astype(F32) + v.astype(F32)).astype(BF16)

    def c2(h):
        slot = rem(h, DEP)

        @pl.when(h >= DEP)
        def _():
            sent(slot, h - DEP)

        done(RB.at[slot], rb_r.at[slot])
        SS[slot] = (PO[...] + RB[slot].astype(F32)).astype(BF16)
        s = ss_s.at[slot]

        def z_way():
            send(SS.at[slot, part(zo, 0)], Z2.at[slot, 0], s, rz2m_r.at[slot], up)
            send(SS.at[slot, part(zo, 1)], Z2.at[slot, 1], s, rz2p_r.at[slot], down)
            send(SS.at[slot, part(zn, 1)], Z1.at[slot, 0, pl.ds(32, 32)], s, rz1m_r.at[slot], up)
            send(SS.at[slot, part(zp_, 0)], Z1.at[slot, 1, pl.ds(0, 32)], s, rz1p_r.at[slot], down)

        def y_way():
            send(SS.at[slot, part(0, 1 - yh, 128)], YB.at[slot], s, ry_r.at[slot], across)

        either(h, z_way, y_way)

    def c3(h):
        slot = rem(h, DEP)
        s = ss_s.at[slot]

        def z_way():
            done(Z2.at[slot, 0], rz2m_r.at[slot])
            b = part(zn, 0)
            add_into(slot, b, Z2[slot, 0])
            send(SS.at[slot, b], Z1.at[slot, 0, pl.ds(0, 32)], s, rz1m_r.at[slot], up)
            done(Z2.at[slot, 1], rz2p_r.at[slot])
            b = part(zp_, 1)
            add_into(slot, b, Z2[slot, 1])
            send(SS.at[slot, b], Z1.at[slot, 1, pl.ds(32, 32)], s, rz1p_r.at[slot], down)

        def y_way():
            done(YB.at[slot], ry_r.at[slot])
            add_into(slot, part(0, yh, 128), YB[slot])
            send(SS.at[slot, part(zo, yh, 16)], Z2.at[slot, 0, pl.ds(0, 16)], s, rz2m_r.at[slot], up)
            send(SS.at[slot, part(zo, yh, 16, 16)], Z2.at[slot, 1, pl.ds(0, 16)], s, rz2p_r.at[slot], down)
            send(SS.at[slot, part(zn, yh, 16, 16)], Z1.at[slot, 0, pl.ds(16, 16)], s, rz1m_r.at[slot], up)
            send(SS.at[slot, part(zp_, yh, 16)], Z1.at[slot, 1, pl.ds(0, 16)], s, rz1p_r.at[slot], down)

        either(h, z_way, y_way)

    def c4(h):
        slot = rem(h, DEP)
        s = ss_s.at[slot]

        @pl.when((h >= DEP) & jnp.logical_not(y_first(h - DEP)))
        def _():
            done(YS.at[slot], ys_s.at[slot])

        def z_way():
            done(Z1.at[slot, 0], rz1m_r.at[slot])
            done(Z1.at[slot, 1], rz1p_r.at[slot])

            def total(yy):
                b = pl.ds(at16(yy * 32), 32)
                return SS[slot, part(z, yy)].astype(F32) + Z1[slot, 0, b].astype(F32) + Z1[slot, 1, b].astype(F32)

            YS[slot] = total(1 - yh).astype(BF16)
            send(YS.at[slot], YR.at[slot], ys_s.at[slot], yr_r.at[slot], across)
            TF[slot] = total(yh)

        def y_way():
            done(Z2.at[slot, 0, pl.ds(0, 16)], rz2m_r.at[slot])
            b = part(zn, yh, 16)
            add_into(slot, b, Z2[slot, 0, 0:16])
            send(SS.at[slot, b], Z1.at[slot, 0, pl.ds(0, 16)], s, rz1m_r.at[slot], up)
            done(Z2.at[slot, 1, pl.ds(0, 16)], rz2p_r.at[slot])
            b = part(zp_, yh, 16, 16)
            add_into(slot, b, Z2[slot, 1, 0:16])
            send(SS.at[slot, b], Z1.at[slot, 1, pl.ds(16, 16)], s, rz1p_r.at[slot], down)

        either(h, z_way, y_way)

    def c5(h):
        slot = rem(h, DEP)

        @pl.when(h >= DEP)
        def _():
            done(EB.at[slot, pl.ds(0, 288)], eb_s.at[slot])

        def z_way():
            done(YR.at[slot], yr_r.at[slot])
            TF[slot] += YR[slot].astype(F32)

        def y_way():
            done(Z1.at[slot, 0, pl.ds(0, 32)], rz1m_r.at[slot])
            done(Z1.at[slot, 1, pl.ds(0, 32)], rz1p_r.at[slot])
            TF[slot] = SS[slot, part(z, yh)].astype(F32) + Z1[slot, 0, 0:32].astype(F32) + Z1[slot, 1, 0:32].astype(F32)

        either(h, z_way, y_way)
        scale = jnp.where(h < NC, gslot[pl.ds(0, 32), :][:, :1], 1.0)
        EB[slot] = dot(A[...], quarters((TF[slot] * scale).astype(BF16))).astype(BF16)
        here = pl.ds(at16(x * 96), 96)
        for p, to in zip(xs, peers):
            send(EB.at[slot, pl.ds(at16(p * 96), 96)], ER.at[slot, here], eb_s.at[slot], er_r.at[slot], to)
        ER[slot, here] = EB[slot, here]

    def c6(h):
        slot = rem(h, DEP)

        @pl.when(h >= DEP)
        def _():
            done(FB.at[slot], fb_s.at[slot])

        done(ER.at[slot, pl.ds(0, 288)], er_r.at[slot])

        def total(yy):
            t = ER[slot, pl.ds(at16(yy * 48, 16), 48)].astype(F32)
            for j in range(1, 4):
                t = t + ER[slot, pl.ds(at16(96 * j + yy * 48, 16), 48)].astype(F32)
            return t

        FB[slot] = total(1 - yl).astype(BF16)
        send(FB.at[slot], FR.at[slot], fb_s.at[slot], fr_r.at[slot], pair)
        FT[slot] = total(yl)

    def c7(h):
        slot = rem(h, DEP)
        done(FR.at[slot], fr_r.at[slot])
        t = FT[slot] + FR[slot].astype(F32)
        t = jnp.concatenate([t[12 * q : 12 * q + 12] for q in range(4)], axis=1).astype(BF16)

        @pl.when(h < NC)
        def _():
            lo_ref[:, pl.ds(at16(h * CW, CW), CW)] = t

        @pl.when(h >= NC)
        def _():
            gt_ref[:, pl.ds(at16((h - NC) * CW, CW), CW)] = t

    def stage(f, i, n=2 * NC):
        @pl.when((i >= 0) & (i < n))
        def _():
            f(i)

    def step(t, carry):
        stage(a1, t + LEAD)
        stage(a2, t)
        stage(a1b, t + 2)
        stage(a3, t - LAG3)
        stage(a4, t - LAG4)
        stage(a5, t - LAG5)
        stage(ay, t - LAGY)
        stage(a6, t - LAG6)
        h = t - OFF
        stage(c7, h - L7)
        stage(c6, h - L6)
        stage(c5, h - L5)
        stage(c4, h - L4)
        stage(c3, h - L3)
        stage(c2, h - L2)
        stage(c1, h)
        return carry

    lax.fori_loop(0, STEPS, step, 0)

    def finish(g, carry):
        done(G.at[g, pl.ds(0, 336)], ge_s.at[g])
        done(R.at[g, pl.ds(0, 480)], ag_s.at[g])
        done(R.at[g], hbm_s.at[g])
        return carry

    lax.fori_loop(0, 2 * NC, finish, 0)
    for i in range(2):
        done(SB.at[i], sb_s.at[i])
    for i in range(2 * NC - DEP, 2 * NC):
        slot = i % DEP
        if y_first(i):
            done(SS.at[slot, pl.ds(0, 224)], ss_s.at[slot])
        else:
            done(SS.at[slot, pl.ds(0, 192)], ss_s.at[slot])
            done(YS.at[slot], ys_s.at[slot])
        done(EB.at[slot, pl.ds(0, 288)], eb_s.at[slot])
        done(FB.at[slot], fb_s.at[slot])


def grads(rows_t, slot_grad, hid_t, gp, gin, gout):
    gin[...] = dot(rows_t[...], gp[...]).astype(BF16)
    for i in range(2):
        gout[:, i * CW : (i + 1) * CW] = dot(hid_t[...], slot_grad[i]).astype(BF16)


def local(tokens, cotangent, expert_ids, gate_values, w_in, w_out):
    vmem, hbm = pl.BlockSpec(memory_space=pltpu.VMEM), pl.BlockSpec(memory_space=pl.ANY)
    dma = lambda n: pltpu.SemaphoreType.DMA((n,))
    layer_out, grad_tokens, rows_t, slot_grad, hid_t, gp = pl.pallas_call(
        exchange,
        name="exchange",
        out_shape=(
            jax.ShapeDtypeStruct((12, D), BF16),
            jax.ShapeDtypeStruct((12, D), BF16),
            jax.ShapeDtypeStruct((D, ROWS), BF16),
            jax.ShapeDtypeStruct((NC, ROWS, CW), BF16),
            jax.ShapeDtypeStruct((ROWS, HID), BF16),
            jax.ShapeDtypeStruct((ROWS, HID), BF16),
        ),
        in_specs=[vmem, vmem, vmem, vmem, hbm, hbm],
        out_specs=(vmem, vmem, hbm, hbm, vmem, vmem),
        scratch_shapes=[
            pltpu.VMEM((D, HID), BF16),
            pltpu.VMEM((HID, D), BF16),
            pltpu.VMEM((2 * NC, 48, QW), BF16),
            pltpu.VMEM((2 * NC, 4 * TOK, QW), BF16),
            pltpu.VMEM((2 * NC, ROWS, CW), BF16),
            pltpu.VMEM((D, ROWS), BF16),
            pltpu.VMEM((ROWS, HID), BF16),
            pltpu.VMEM((ROWS, HID), F32),
            pltpu.VMEM((ROWS, HID), F32),
            pltpu.VMEM((4 * TOK, 128), BF16),
            pltpu.VMEM((128, 4 * TOK), BF16),
            pltpu.VMEM((4 * TOK, 128), F32),
            pltpu.VMEM((128, 128), F32),
            pltpu.VMEM((2, HALF, CW), BF16),
            pltpu.VMEM((HALF, CW), F32),
            pltpu.VMEM((DEP, HALF, CW), BF16),
            pltpu.VMEM((DEP, HALF, CW), BF16),
            pltpu.VMEM((DEP, 2, 32, CW), BF16),
            pltpu.VMEM((DEP, 2, 64, CW), BF16),
            pltpu.VMEM((DEP, 128, CW), BF16),
            pltpu.VMEM((DEP, 32, CW), BF16),
            pltpu.VMEM((DEP, 32, CW), BF16),
            pltpu.VMEM((DEP, 32, CW), F32),
            pltpu.VMEM((DEP, 4 * TOK, QW), BF16),
            pltpu.VMEM((DEP, 4 * TOK, QW), BF16),
            pltpu.VMEM((DEP, 48, QW), BF16),
            pltpu.VMEM((DEP, 48, QW), BF16),
            pltpu.VMEM((DEP, 48, QW), F32),
            dma(2),
        ]
        + [dma(2 * NC) for _ in range(11)]
        + [dma(2), dma(DEP), dma(DEP)]
        + [dma(DEP) for _ in range(11)],
        compiler_params=pltpu.CompilerParams(
            collective_id=0, has_side_effects=True, vmem_limit_bytes=56 * 2**20
        ),
    )(tokens, cotangent, expert_ids.T, gate_values.T, w_in[0], w_out[0])
    grad_in, grad_out = pl.pallas_call(
        grads,
        name="grads",
        grid=(NC // 2,),
        out_shape=(
            jax.ShapeDtypeStruct((D, HID), BF16),
            jax.ShapeDtypeStruct((HID, D), BF16),
        ),
        in_specs=[
            pl.BlockSpec((2 * CW, ROWS), lambda k: (k, 0)),
            pl.BlockSpec((2, ROWS, CW), lambda k: (k, 0, 0)),
            pl.BlockSpec((ROWS, HID), lambda k: (0, 0)),
            pl.BlockSpec((ROWS, HID), lambda k: (0, 0)),
        ],
        out_specs=(
            pl.BlockSpec((2 * CW, HID), lambda k: (k, 0)),
            pl.BlockSpec((HID, 2 * CW), lambda k: (0, k)),
        ),
        compiler_params=pltpu.CompilerParams(vmem_limit_bytes=62 * 2**20),
    )(rows_t, slot_grad, hid_t, gp)
    return layer_out, grad_tokens, grad_in[None], grad_out[None]


def solution(mesh):
    placed = (
        P(("dp", "expert"), None),
        P(("dp", "expert"), None),
        P("dp", None),
        P("dp", None),
        P("expert", None, "dp"),
        P("expert", "dp", None),
    )
    return jax.shard_map(
        local,
        mesh=mesh,
        in_specs=placed,
        out_specs=(
            P(("dp", "expert"), None),
            P(("dp", "expert"), None),
            P("expert", None, "dp"),
            P("expert", "dp", None),
        ),
        check_vma=False,
    )
```
